32 devices in a mesh: dp: 4 (over y, core), ctx: 8 (over z, x).
Axes of the slice: x: 2, y: 2, z: 4, core: 2. Of those that a mesh axis runs over, the one named last changes fastest.
Arguments:
- mixer_input: bfloat16 [4096, 2560], P(('dp', 'ctx')), parts along dimension 0, may hold values from -6 to 6
- input_map: bfloat16 [4096, 128], P(('dp', 'ctx')), parts along dimension 0, may hold values from -6 to 6
- output_map: bfloat16 [4096, 128], P(('dp', 'ctx')), parts along dimension 0, may hold values from -0.03125 to 0.03125
- log_decay: float32 [4096, 40], P(('dp', 'ctx')), parts along dimension 0, may hold values from -1 to 0
- query_rows: bfloat16 [4096, 2560], P(('dp', 'ctx')), parts along dimension 0, may hold values from -7 to 7
- key_rows: bfloat16 [4096, 320], P(('dp', 'ctx')), parts along dimension 0, may hold values from -7 to 7
- value_rows: bfloat16 [4096, 320], P(('dp', 'ctx')), parts along dimension 0, may hold values from -6 to 6
Outputs:
- mixer_output: bfloat16 [4096, 2560], P(('dp', 'ctx')), parts along dimension 0
- attention_output: bfloat16 [4096, 2560], P(('dp', 'ctx')), parts along dimension 0
The draws below stay inside these ranges and needn't reach their ends.
There are 4 independent parts, one for each index of `dp`. The reference program is written for one: setup_inputs(seed, part) draws one part's arguments, and reference() takes and returns one part's arrays. A program takes and returns all parts, laid end to end along the dimension named above; each array names one. Nothing has to cross between parts.
All inputs are finite; a program needn't handle non-finite values.
Results may differ from the reference program's by a relative error of at most 0.0049.
Values may be sent and summed in bfloat16 or wider, within the bound.
A program may use at most 128 MiB of HBM per device.

```python
import math
import jax
import jax.numpy as jnp
from jax import lax

MIXER_HEADS = 40
P_SIZE = 64
N = 128
QH = 32
KVH = 4
DH = 80
STRETCH = 128
TOK_DEV = 128
SEQUENCE_LENGTH = 1024


def draw_query_rows(key, part):
    base = jax.random.fold_in(key, 1)
    values = jnp.clip(jax.random.normal(base, (SEQUENCE_LENGTH, QH * DH), jnp.float32), -6.0, 6.0)
    return values.astype(jnp.bfloat16)


def draw_key_rows(key, part):
    base = jax.random.fold_in(key, 2)
    values = jnp.clip(jax.random.normal(base, (SEQUENCE_LENGTH, KVH * DH), jnp.float32), -6.0, 6.0)
    return values.astype(jnp.bfloat16)


def draw_log_decay(key, part):
    random_keys = jax.random.split(jax.random.fold_in(key, 5), 7)
    slow_share = 0.6
    picked = jax.random.uniform(random_keys[0], (MIXER_HEADS,), jnp.float32) < slow_share
    slow_rate = jnp.exp(jax.random.uniform(random_keys[1], (MIXER_HEADS,), jnp.float32, math.log(0.1 / SEQUENCE_LENGTH), math.log(0.5 / SEQUENCE_LENGTH)))
    fast_rate = jnp.exp(jax.random.uniform(random_keys[2], (MIXER_HEADS,), jnp.float32, math.log(0.5 / SEQUENCE_LENGTH), math.log(0.04)))
    event_rate = jnp.where(picked, slow_rate, fast_rate)
    device_multiplier = jax.random.uniform(random_keys[3], (SEQUENCE_LENGTH // TOK_DEV, 1, MIXER_HEADS), jnp.float32, 0.5, 1.5)
    device_multiplier = jnp.broadcast_to(device_multiplier, (SEQUENCE_LENGTH // TOK_DEV, TOK_DEV, MIXER_HEADS)).reshape(SEQUENCE_LENGTH, MIXER_HEADS)
    coarse_estimate = jax.random.uniform(random_keys[4], (SEQUENCE_LENGTH, MIXER_HEADS), jnp.float32, 0.5, 1.5)
    third_portion = SEQUENCE_LENGTH // 3
    spurt_location = jnp.arange(3, dtype=jnp.int32) * third_portion + jax.random.randint(random_keys[5], (3,), 0, third_portion)
    spurt_retain = jnp.log(jax.random.uniform(random_keys[6], (3, MIXER_HEADS), jnp.float32, 0.5, 0.8))
    match_count = (jnp.arange(SEQUENCE_LENGTH, dtype=jnp.int32)[:, None] == spurt_location[None, :]).astype(jnp.float32)
    spurt_list = jnp.sum(match_count[:, :, None] * spurt_retain[None], axis=1)
    return -event_rate[None, :] * device_multiplier * coarse_estimate + spurt_list


def shard_levels(own_key, dims, pieces, least, top_value):
    def one(dim, blocks):
        heights = jax.random.uniform(jax.random.fold_in(jax.random.fold_in(own_key, 6), dim), (blocks,), jnp.float32, least / len(pieces), top_value / len(pieces))
        return jnp.repeat(jnp.exp(heights), dims[dim] // blocks).reshape((-1,) + (1,) * (len(dims) - dim - 1))

    factor_of = one(*pieces[0])
    for cut in pieces[1:]:
        factor_of = factor_of * one(*cut)
    return factor_of


def scatter_about(rng, shape, spread, reach, shards=(), kind=jnp.bfloat16):
    entries = jax.random.normal(rng, shape, jnp.float32) * spread
    if len(shards) > 0:
        entries = shard_levels(rng, shape, shards, -0.22, 0.18) * entries
    return jnp.clip(entries, min=-reach, max=reach).astype(kind)


def setup_inputs(seed: int = 0, part: int = 0) -> dict:
    splits = jax.random.split(jax.random.key(seed), 8)
    own_keys = jax.random.split(jax.random.fold_in(splits[7], part), 8)
    mixer_input = scatter_about(own_keys[0], (SEQUENCE_LENGTH, MIXER_HEADS * P_SIZE), 1.0, 6.0, ((0, 8),))
    input_map = scatter_about(own_keys[1], (SEQUENCE_LENGTH, N), 1.0, 6.0, ((0, 8),))
    output_map = scatter_about(own_keys[2], (SEQUENCE_LENGTH, N), (N * SEQUENCE_LENGTH // 4) ** -0.5, 0.03125, ((0, 8),))
    log_decay = draw_log_decay(jax.random.fold_in(jax.random.fold_in(splits[7], part), 71), part)
    query_rows = draw_query_rows(jax.random.fold_in(jax.random.fold_in(splits[7], part), 71), part)
    key_rows = draw_key_rows(jax.random.fold_in(jax.random.fold_in(splits[7], part), 71), part)
    value_rows = scatter_about(own_keys[6], (SEQUENCE_LENGTH, KVH * DH), 1.0, 6.0, ((0, 8),))
    return dict(mixer_input=mixer_input, input_map=input_map, output_map=output_map, log_decay=log_decay, query_rows=query_rows, key_rows=key_rows, value_rows=value_rows)


masked_score = -1e+30

def mixer_part(mixer_input, input_map, output_map, log_decay):
    length = mixer_input.shape[0]
    count = length // STRETCH
    x_blocks = mixer_input.reshape(count, STRETCH, MIXER_HEADS, P_SIZE)
    in_blocks = input_map.reshape(count, STRETCH, N)
    out_blocks = output_map.reshape(count, STRETCH, N)
    decay_blocks = log_decay.reshape(count, STRETCH, MIXER_HEADS)
    lower_mask = jnp.tril(jnp.ones((STRETCH, STRETCH), dtype=bool))

    def advance(state, items):
        x_block, in_block, out_block, decay_block = items
        cumulative = jnp.cumsum(decay_block, axis=0).T
        match = jnp.dot(out_block, in_block.T, preferred_element_type=jnp.float32)
        decay_gap = jnp.where(lower_mask[None], cumulative[:, :, None] - cumulative[:, None, :], 0.0)
        weights = jnp.where(lower_mask[None], match[None] * jnp.exp(decay_gap), 0.0).astype(jnp.bfloat16)
        inner = jnp.einsum('hts,shp->thp', weights.astype(jnp.float32), x_block.astype(jnp.float32))
        carried = jnp.einsum('tn,hnp->thp', out_block.astype(jnp.float32), state, precision=lax.Precision.HIGHEST)
        carried = carried * jnp.exp(cumulative).T[:, :, None]
        result = (inner + carried).astype(jnp.bfloat16)
        weighted = (jnp.exp(cumulative[:, -1:] - cumulative)[:, :, None] * in_block.astype(jnp.float32)[None]).astype(jnp.bfloat16)
        update = jnp.einsum('hsn,shp->hnp', weighted.astype(jnp.float32), x_block.astype(jnp.float32))
        state = jnp.exp(cumulative[:, -1])[:, None, None] * state + update
        return (state, result)
    start_state = jnp.zeros((MIXER_HEADS, N, P_SIZE), jnp.float32)
    unused, results = lax.scan(advance, start_state, (x_blocks, in_blocks, out_blocks, decay_blocks))
    return results.reshape(length, MIXER_HEADS * P_SIZE)

def attention_part(query_rows, key_rows, value_rows):
    length = query_rows.shape[0]
    group = QH // KVH
    scale = 1.0 / math.sqrt(DH)
    causal = jnp.tril(jnp.ones((length, length), dtype=bool))

    def one_head(head):
        kv_head = head // group
        query_cols = lax.dynamic_slice_in_dim(query_rows, (head * DH).astype(jnp.int32), DH, 1)
        key_cols = lax.dynamic_slice_in_dim(key_rows, (kv_head * DH).astype(jnp.int32), DH, 1)
        value_cols = lax.dynamic_slice_in_dim(value_rows, (kv_head * DH).astype(jnp.int32), DH, 1)
        scores = jnp.dot(query_cols, key_cols.T, preferred_element_type=jnp.float32) * scale
        scores = jnp.where(causal, scores, masked_score)
        top = lax.optimization_barrier(jnp.max(scores, axis=-1, keepdims=True))
        expo = jnp.exp(scores - top)
        total = lax.optimization_barrier(jnp.sum(expo, axis=-1, keepdims=True))
        summed = jnp.dot(expo.astype(jnp.bfloat16), value_cols, preferred_element_type=jnp.float32)
        return (summed / total).astype(jnp.bfloat16)
    outputs = lax.map(one_head, jnp.arange(QH, dtype=jnp.int32))
    return outputs.transpose(1, 0, 2).reshape(length, QH * DH)

def reference(mixer_input, input_map, output_map, log_decay, query_rows, key_rows, value_rows):
    mixer_output = mixer_part(mixer_input, input_map, output_map, log_decay)
    attention_output = attention_part(query_rows, key_rows, value_rows)
    return (mixer_output, attention_output)
```

```python
import functools
import math

import jax
import jax.numpy as jnp
from jax import lax
from jax.experimental import pallas as pl
from jax.experimental.pallas import tpu as pltpu
from jax.sharding import PartitionSpec as P

MIXER_HEADS = 40
P_SIZE = 64
N = 128
QH = 32
KVH = 4
DH = 80
T = 128
GROUP = QH // KVH
CHUNKS = 5
CW = 256
PAIRS = MIXER_HEADS // 2
SCALE = 1.0 / math.sqrt(DH)
MASKED = -1e30
MESH = pl.DeviceIdType.MESH
BF = jnp.bfloat16
F32 = jnp.float32
VMEM_LIMIT = 56 * 1024 * 1024


def iota(shape, dim):
    return lax.broadcasted_iota(jnp.int32, shape, dim)


def nt_dot(a, b):
    return lax.dot_general(a, b, (((1,), (1,)), ((), ())), preferred_element_type=F32)


def dot(a, b):
    return jnp.dot(a, b, preferred_element_type=F32)


def local_kernel(x_ref, in_ref, out_ref, ld_ref, k_ref, v_ref, u_ref, f_ref, inner_ref, ecum_ref, kv_ref):
    kv_ref[:, : KVH * DH] = k_ref[...]
    kv_ref[:, KVH * DH :] = v_ref[...]
    lower = iota((T, T), 0) >= iota((T, T), 1)
    tril = jnp.where(lower, 1.0, 0.0).astype(F32)
    cum = jnp.dot(tril, ld_ref[...], precision=lax.Precision.HIGHEST, preferred_element_type=F32)
    cum_t = jnp.concatenate([cum, jnp.zeros((T, T - MIXER_HEADS), F32)], axis=1).T
    ecum = jnp.exp(cum)
    ecum_ref[...] = ecum
    match = jnp.where(lower, nt_dot(out_ref[...], in_ref[...]), 0.0)
    in_t = in_ref[...].astype(F32).T
    left = iota((T, T), 1) < P_SIZE
    for j in range(PAIRS):
        stack = []
        tails = []
        for h in (2 * j, 2 * j + 1):
            row = cum_t[h : h + 1, :]
            gap = jnp.minimum(cum[:, h : h + 1] - row, 0.0)
            stack.append((match * jnp.exp(gap)).astype(BF))
            tails.append((in_t * jnp.exp(cum[T - 1 : T, h : h + 1] - row)).astype(BF))
        out = dot(jnp.concatenate(stack + tails, axis=0), x_ref[:, j * T : (j + 1) * T])
        inner_ref[:, j * T : (j + 1) * T] = jnp.where(left, out[:T], out[T : 2 * T])
        half, place = divmod(j, PAIRS // 2)
        c, lane = divmod(place * T, CW)
        u_ref[half, c, :, lane : lane + T] = jnp.where(left, out[2 * T : 3 * T], out[3 * T :])
        last = ecum[T - 1 : T, :]
        f_ref[half, :, place * T : (place + 1) * T] = jnp.where(
            left[:1], last[:, 2 * j : 2 * j + 1], last[:, 2 * j + 1 : 2 * j + 2]
        )


def exchange_kernel(
    n, u_ref, f_ref, kv_ref, kvall_ref, ent_ref,
    own, usend, urecv, frecv, sin, sout, entsend,
    us_sem, ur_sem, f_sem, ss_sem, sr_sem, es_sem, er_sem, kvs_sem, kvr_sem, px_sem, loc_sem,
):
    dp = lax.axis_index("dp")
    me = lax.axis_index("ctx")
    a, b = me // 2, me % 2
    rows = n // 2
    partner = (dp, a * 2 + 1 - b)

    barrier = pltpu.get_barrier_semaphore()
    pl.semaphore_signal(barrier, inc=1, device_id=partner, device_id_type=MESH)
    for d in range(1, rows):
        pl.semaphore_signal(
            barrier, inc=1, device_id=(dp, lax.rem(a + d, rows) * 2 + b), device_id_type=MESH
        )
    pl.semaphore_wait(barrier, rows)

    def ucopy(c):
        return pltpu.make_async_remote_copy(
            src_ref=usend.at[c], dst_ref=urecv.at[c], send_sem=us_sem.at[c],
            recv_sem=ur_sem.at[c], device_id=partner, device_id_type=MESH)

    def fcopy():
        return pltpu.make_async_remote_copy(
            src_ref=f_ref.at[1 - b], dst_ref=frecv, send_sem=f_sem.at[0],
            recv_sem=f_sem.at[1], device_id=partner, device_id_type=MESH)

    def scopy(c):
        return pltpu.make_async_remote_copy(
            src_ref=sout.at[c], dst_ref=sin.at[c], send_sem=ss_sem.at[c],
            recv_sem=sr_sem.at[c], device_id=(dp, (a + 1) * 2 + b), device_id_type=MESH)

    def ecopy(c):
        return pltpu.make_async_remote_copy(
            src_ref=entsend.at[c], dst_ref=ent_ref.at[b, c], send_sem=es_sem.at[c],
            recv_sem=er_sem.at[c], device_id=partner, device_id_type=MESH)

    def kvcopy(d):
        return pltpu.make_async_remote_copy(
            src_ref=own, dst_ref=kvall_ref.at[me], send_sem=kvs_sem.at[d],
            recv_sem=kvr_sem.at[me], device_id=(dp, (a + d) * 2 + b), device_id_type=MESH)

    def kvforward(d, block):
        return pltpu.make_async_remote_copy(
            src_ref=kvall_ref.at[block], dst_ref=kvall_ref.at[block], send_sem=px_sem.at[d],
            recv_sem=kvr_sem.at[block], device_id=partner, device_id_type=MESH)

    def kvarrive(block):
        return pltpu.make_async_copy(kvall_ref.at[block], kvall_ref.at[block], kvr_sem.at[block])

    fcopy().start()
    for c in range(CHUNKS):
        usend[c] = u_ref[1 - b, c].astype(BF)
        ucopy(c).start()
    own[...] = kv_ref[...]
    kvall_ref[me] = kv_ref[...]

    @pl.when(b == 0)
    def _():
        kvforward(0, me).start()
        kvall_ref[me + 1] = jnp.zeros((T, 2 * KVH * DH), BF)

    for d in range(1, rows):
        @pl.when(a + d < rows)
        def _():
            kvcopy(d).start()

    fcopy().wait_recv()
    first = b == 0
    f_own = f_ref[b]
    f_other = frecv[...]
    f_early = jnp.where(first, f_own, f_other)
    f_late = jnp.where(first, f_other, f_own)
    f_pair = f_early * f_late

    for c in range(CHUNKS):
        lanes = slice(c * CW, (c + 1) * CW)
        ucopy(c).wait_recv()
        u_own = u_ref[b, c]
        u_other = urecv[c].astype(F32)
        early = jnp.where(first, u_own, u_other)
        late = jnp.where(first, u_other, u_own)
        pair = f_late[:, lanes] * early + late

        @pl.when(a == 0)
        def _():
            sin[c] = jnp.zeros((T, CW), BF)

        @pl.when(a > 0)
        def _():
            scopy(c).wait_recv()

        state = sin[c].astype(F32)

        @pl.when(a + 1 < rows)
        def _():
            sout[c] = (f_pair[:, lanes] * state + pair).astype(BF)
            scopy(c).start()

        middle = f_early[:, lanes] * state + early
        entsend[c] = jnp.where(first, middle, state).astype(BF)
        ecopy(c).start()
        ent_ref[b, c] = jnp.where(first, state, middle).astype(BF)

        if c + 1 < rows:
            d = c + 1

            @pl.when(a - d >= 0)
            def _():
                kvarrive(me - 2 * d).wait()
                kvforward(d, me - 2 * d).start()

    for d in range(CHUNKS + 1, rows):
        @pl.when(a - d >= 0)
        def _():
            kvarrive(me - 2 * d).wait()
            kvforward(d, me - 2 * d).start()

    for d in range(rows):
        block = (a - d) * 2 + 1 - b
        valid = (a - d >= 0) if d > 0 else (b == 1)

        @pl.when(valid)
        def _():
            kvarrive(block).wait()

    for c in range(CHUNKS):
        ucopy(c).wait_send()
        ecopy(c).wait_send()
        ecopy(c).wait_recv()

        @pl.when(a + 1 < rows)
        def _():
            scopy(c).wait_send()
    fcopy().wait_send()

    @pl.when(b == 0)
    def _():
        kvforward(0, me).wait_send()

    for d in range(1, rows):
        @pl.when(a + d < rows)
        def _():
            kvcopy(d).wait_send()

        @pl.when(a - d >= 0)
        def _():
            kvforward(d, me - 2 * d).wait_send()


def attend_group(n, g, a, b, q_ref, kvall_ref, att_ref, qs, ks, vs, sc, top, total, acc):
    wide = 2 * T
    for r in range(GROUP):
        h = g * GROUP + r
        qs[r * T : (r + 1) * T, :] = q_ref[:, h * DH : (h + 1) * DH]
    kc = g * DH
    vc = (KVH + g) * DH

    def fill(p, _):
        for e in range(2):
            at = pl.ds(pl.multiple_of(p * wide + e * T, T), T)
            ks[at, :] = kvall_ref[2 * p + e, :, kc : kc + DH]
            vs[at, :] = kvall_ref[2 * p + e, :, vc : vc + DH]
        return 0

    lax.fori_loop(0, a + 1, fill, 0)
    chunk = 2 * T
    parts = GROUP * T // chunk

    def visible():
        return iota((chunk, wide), 1) <= (iota((chunk, wide), 0) % T) + b * T

    at = pl.ds(pl.multiple_of(a * wide, wide), wide)
    for r in range(parts):
        rows = slice(r * chunk, (r + 1) * chunk)
        s = nt_dot(qs[rows, :], ks[at, :]) * SCALE
        s = jnp.where(visible(), s, MASKED)
        sc[a, rows, :] = s
        top[rows, :] = jnp.maximum(s[:, :T], s[:, T:])

    def score(p, _):
        at = pl.ds(pl.multiple_of(p * wide, wide), wide)
        for r in range(parts):
            rows = slice(r * chunk, (r + 1) * chunk)
            s = nt_dot(qs[rows, :], ks[at, :]) * SCALE
            sc[p, rows, :] = s
            top[rows, :] = jnp.maximum(top[rows, :], jnp.maximum(s[:, :T], s[:, T:]))
        return 0

    lax.fori_loop(0, a, score, 0)
    for r in range(parts):
        rows = slice(r * chunk, (r + 1) * chunk)
        peak = jnp.max(top[rows, :], axis=1, keepdims=True)
        top[rows, :] = jnp.broadcast_to(peak, (chunk, T))
        total[rows, :] = jnp.zeros((chunk, T), F32)
        acc[rows, :] = jnp.zeros((chunk, DH), F32)

    def gather(p, _):
        at = pl.ds(pl.multiple_of(p * wide, wide), wide)
        for r in range(parts):
            rows = slice(r * chunk, (r + 1) * chunk)
            peak = top[rows, :]
            e0 = jnp.exp(sc[p, rows, :T] - peak)
            e1 = jnp.exp(sc[p, rows, T:] - peak)
            total[rows, :] += e0 + e1
            e = jnp.concatenate([e0.astype(BF), e1.astype(BF)], axis=1)
            acc[rows, :] += dot(e, vs[at, :])
        return 0

    lax.fori_loop(0, a + 1, gather, 0)
    outs = []
    for r in range(GROUP):
        rows = slice(r * T, (r + 1) * T)
        outs.append((acc[rows, :] / jnp.sum(total[rows, :], axis=1, keepdims=True)).astype(BF))
    wide_out = GROUP * DH
    att_ref[:, g * wide_out : (g + 1) * wide_out] = jnp.concatenate(outs, axis=1)


def finish_kernel(n, q_ref, kvall_ref, out_ref, ent_ref, inner_ref, ecum_ref, mix_ref, att_ref, *scratch):
    me = lax.axis_index("ctx")
    a, b = me // 2, me % 2
    for g in range(KVH):
        attend_group(n, g, a, b, q_ref, kvall_ref, att_ref, *scratch)
    left = iota((T, T), 1) < P_SIZE
    for half in range(2):
        for c in range(CHUNKS):
            carried = dot(out_ref[...], ent_ref[half, c])
            for e in range(CW // T):
                j = (half * CHUNKS + c) * (CW // T) + e
                factor = jnp.where(
                    left, ecum_ref[:, 2 * j : 2 * j + 1], ecum_ref[:, 2 * j + 1 : 2 * j + 2]
                )
                cols = slice(j * T, (j + 1) * T)
                mix_ref[:, cols] = (
                    inner_ref[:, cols] + carried[:, e * T : (e + 1) * T] * factor
                ).astype(BF)


def specs(count):
    return [pl.BlockSpec(memory_space=pltpu.VMEM)] * count


def per_device(n, mixer_input, input_map, output_map, log_decay, query_rows, key_rows, value_rows):
    width = MIXER_HEADS * P_SIZE
    u, f, inner, ecum, kv = pl.pallas_call(
        local_kernel,
        out_shape=(
            jax.ShapeDtypeStruct((2, CHUNKS, N, CW), F32),
            jax.ShapeDtypeStruct((2, 1, width // 2), F32),
            jax.ShapeDtypeStruct((T, width), F32),
            jax.ShapeDtypeStruct((T, MIXER_HEADS), F32),
            jax.ShapeDtypeStruct((T, 2 * KVH * DH), BF),
        ),
        in_specs=specs(6),
        out_specs=specs(5),
        compiler_params=pltpu.CompilerParams(vmem_limit_bytes=VMEM_LIMIT),
        name="local",
    )(mixer_input, input_map, output_map, log_decay, key_rows, value_rows)
    rows = n // 2
    sem = pltpu.SemaphoreType.DMA
    chunked = pltpu.VMEM((CHUNKS, N, CW), BF)
    kvall, ent = pl.pallas_call(
        functools.partial(exchange_kernel, n),
        out_shape=(
            jax.ShapeDtypeStruct((n, T, 2 * KVH * DH), BF),
            jax.ShapeDtypeStruct((2, CHUNKS, N, CW), BF),
        ),
        in_specs=specs(3),
        out_specs=specs(2),
        scratch_shapes=[
            pltpu.VMEM((T, 2 * KVH * DH), BF),
            chunked, chunked, pltpu.VMEM((1, width // 2), F32), chunked, chunked, chunked,
            sem((CHUNKS,)), sem((CHUNKS,)), sem((2,)), sem((CHUNKS,)), sem((CHUNKS,)),
            sem((CHUNKS,)), sem((CHUNKS,)), sem((rows,)), sem((n,)), sem((rows,)), sem((1,)),
        ],
        compiler_params=pltpu.CompilerParams(
            collective_id=0, has_side_effects=True, vmem_limit_bytes=VMEM_LIMIT
        ),
        name="exchange",
    )(u, f, kv)
    big = GROUP * T
    return pl.pallas_call(
        functools.partial(finish_kernel, n),
        out_shape=(
            jax.ShapeDtypeStruct((T, width), BF),
            jax.ShapeDtypeStruct((T, QH * DH), BF),
        ),
        in_specs=specs(6),
        out_specs=specs(2),
        scratch_shapes=[
            pltpu.VMEM((big, DH), BF),
            pltpu.VMEM((n * T, DH), BF),
            pltpu.VMEM((n * T, DH), BF),
            pltpu.VMEM((rows, big, 2 * T), F32),
            pltpu.VMEM((big, T), F32),
            pltpu.VMEM((big, T), F32),
            pltpu.VMEM((big, DH), F32),
        ],
        compiler_params=pltpu.CompilerParams(vmem_limit_bytes=VMEM_LIMIT),
        name="finish",
    )(query_rows, kvall, output_map, ent, inner, ecum)


def solution(mesh):
    rows = P(("dp", "ctx"), None)
    return jax.shard_map(
        functools.partial(per_device, mesh.shape["ctx"]),
        mesh=mesh,
        in_specs=(rows,) * 7,
        out_specs=(rows, rows),
        check_vma=False,
    )
```

```python
import functools
import math

import jax
import jax.numpy as jnp
from jax import lax
from jax.experimental import pallas as pl
from jax.experimental.pallas import tpu as pltpu
from jax.sharding import PartitionSpec as P

MIXER_HEADS = 40
P_SIZE = 64
N = 128
QH = 32
KVH = 4
DH = 80
T = 128
GROUP = QH // KVH
KV_ROWS = 2 * KVH * DH
CHUNKS = 5
CW = 256
PAIRS = MIXER_HEADS // 2
HALF = MIXER_HEADS * P_SIZE // 2
EXP_SCALE = math.log2(math.e) / math.sqrt(DH)
MASKED = -1e30
MESH = pl.DeviceIdType.MESH
BF = jnp.bfloat16
F32 = jnp.float32
VMEM_LIMIT = 56 * 1024 * 1024


def iota(shape, dim):
    return lax.broadcasted_iota(jnp.int32, shape, dim)


def nt_dot(a, b):
    return lax.dot_general(a, b, (((1,), (1,)), ((), ())), preferred_element_type=F32)


def dot(a, b):
    return jnp.dot(a, b, preferred_element_type=F32)


def kernel(
    n, x_ref, in_ref, out_ref, ld_ref, q_ref, k_ref, v_ref, mix_ref, att_ref,
    kvall, u, f, inner, ecum_ref, usend, urecv, frecv, sin, sout, entsend, ent,
    qs, top, total, acc,
    us_sem, ur_sem, f_sem, ss_sem, sr_sem, es_sem, er_sem, kvs_sem, kvr_sem, px_sem,
):
    dp = lax.axis_index("dp")
    me = lax.axis_index("ctx")
    a, b = me // 2, me % 2
    rows = n // 2
    partner = (dp, a * 2 + 1 - b)
    ahead = (dp, lax.rem(a + 1, rows) * 2 + b)
    behind = (dp, lax.rem(a + rows - 1, rows) * 2 + b)
    first = b == 0

    def ucopy(c):
        return pltpu.make_async_remote_copy(
            src_ref=usend.at[c], dst_ref=urecv.at[c], send_sem=us_sem.at[c],
            recv_sem=ur_sem.at[c], device_id=partner, device_id_type=MESH)

    def fcopy():
        return pltpu.make_async_remote_copy(
            src_ref=f.at[1 - b], dst_ref=frecv, send_sem=f_sem.at[0],
            recv_sem=f_sem.at[1], device_id=partner, device_id_type=MESH)

    def scopy(c):
        return pltpu.make_async_remote_copy(
            src_ref=sout.at[c], dst_ref=sin.at[c], send_sem=ss_sem.at[c],
            recv_sem=sr_sem.at[c], device_id=ahead, device_id_type=MESH)

    def ecopy(c):
        return pltpu.make_async_remote_copy(
            src_ref=entsend.at[c], dst_ref=ent.at[b, c], send_sem=es_sem.at[c],
            recv_sem=er_sem.at[c], device_id=partner, device_id_type=MESH)

    def kvhop(d):
        block = me - 2 * d
        return pltpu.make_async_remote_copy(
            src_ref=kvall.at[block], dst_ref=kvall.at[block], send_sem=kvs_sem.at[d],
            recv_sem=kvr_sem.at[block], device_id=ahead, device_id_type=MESH)

    def kvside(d):
        block = me - 2 * d
        return pltpu.make_async_remote_copy(
            src_ref=kvall.at[block], dst_ref=kvall.at[block], send_sem=px_sem.at[d],
            recv_sem=kvr_sem.at[block], device_id=partner, device_id_type=MESH)

    def kvarrive(block):
        pltpu.make_async_copy(kvall.at[block], kvall.at[block], kvr_sem.at[block]).wait()

    barrier = pltpu.get_barrier_semaphore()
    for device in (partner, ahead, behind):
        pl.semaphore_signal(barrier, inc=1, device_id=device, device_id_type=MESH)
    kvall[me, : KVH * DH, :] = k_ref[...]
    kvall[me, KVH * DH :, :] = v_ref[...]
    pl.semaphore_wait(barrier, 3)

    @pl.when(a + 1 < rows)
    def _():
        kvhop(0).start()

    lower = iota((T, T), 0) >= iota((T, T), 1)
    triu = jnp.where(iota((T, T), 0) <= iota((T, T), 1), 1.0, 0.0).astype(F32)
    cum_t = jnp.dot(ld_ref[...], triu, precision=lax.Precision.HIGHEST, preferred_element_type=F32)
    cum = jnp.concatenate([cum_t, jnp.zeros((T - MIXER_HEADS, T), F32)], axis=0).T
    ecum = jnp.exp(cum)
    ecum_ref[...] = ecum
    match = jnp.where(lower, nt_dot(out_ref[...], in_ref[...]), 0.0)
    in_t = in_ref[...].astype(F32).T
    left = iota((T, T), 1) < P_SIZE
    last = ecum[T - 1 : T, :]
    for j in range(PAIRS):
        half, place = divmod(j, PAIRS // 2)
        f[half, :, place * T : (place + 1) * T] = jnp.where(
            left[:1], last[:, 2 * j : 2 * j + 1], last[:, 2 * j + 1 : 2 * j + 2]
        )
    fcopy().start()
    for c in range(CHUNKS):
        for half in range(2):
            for e in range(CW // T):
                j = (half * CHUNKS + c) * (CW // T) + e
                stack = []
                tails = []
                for h in (2 * j, 2 * j + 1):
                    row = cum_t[h : h + 1, :]
                    gap = jnp.minimum(cum[:, h : h + 1] - row, 0.0)
                    stack.append((match * jnp.exp(gap)).astype(BF))
                    tails.append((in_t * jnp.exp(row[:, T - 1 :] - row)).astype(BF))
                cols = slice(j * T, (j + 1) * T)
                out = dot(jnp.concatenate(stack + tails, axis=0), x_ref[:, cols])
                inner[:, cols] = jnp.where(left, out[:T], out[T : 2 * T])
                u[half, c, :, e * T : (e + 1) * T] = jnp.where(
                    left, out[2 * T : 3 * T], out[3 * T :]
                )
        usend[c] = u[1 - b, c].astype(BF)
        ucopy(c).start()
        if c == 0:
            @pl.when(first)
            def _():
                kvside(0).start()

    @pl.when(first)
    def _():
        kvall[me + 1] = jnp.zeros((KV_ROWS, T), BF)

    def hand_on(d):
        @pl.when(a - d >= 0)
        def _():
            kvarrive(me - 2 * d)
            kvside(d).start()

            @pl.when(a + 1 < rows)
            def _():
                kvhop(d).start()

    def chain():
        fcopy().wait_recv()
        f_own = f[b]
        f_other = frecv[...]
        f_early = jnp.where(first, f_own, f_other)
        f_late = jnp.where(first, f_other, f_own)
        f_pair = f_early * f_late
        for c in range(CHUNKS):
            lanes = slice(c * CW, (c + 1) * CW)
            ucopy(c).wait_recv()
            u_own = u[b, c]
            u_other = urecv[c].astype(F32)
            early = jnp.where(first, u_own, u_other)
            late = jnp.where(first, u_other, u_own)
            pair = f_late[:, lanes] * early + late

            @pl.when(a == 0)
            def _():
                sin[c] = jnp.zeros((T, CW), BF)

            @pl.when(a > 0)
            def _():
                scopy(c).wait_recv()

            state = sin[c].astype(F32)

            @pl.when(a + 1 < rows)
            def _():
                sout[c] = (f_pair[:, lanes] * state + pair).astype(BF)
                scopy(c).start()

            middle = f_early[:, lanes] * state + early
            entsend[c] = jnp.where(first, middle, state).astype(BF)
            ecopy(c).start()
            ent[b, c] = jnp.where(first, state, middle).astype(BF)

    chunk = 2 * T
    parts = GROUP * T // chunk

    def attend(p, opening):
        def group(g, _):
            kc = pl.ds(pl.multiple_of(g * DH, 16), DH)
            vc = pl.ds(pl.multiple_of((KVH + g) * DH, 16), DH)
            keys = jnp.concatenate([kvall[2 * p, kc, :], kvall[2 * p + 1, kc, :]], axis=1)
            values = jnp.concatenate([kvall[2 * p, vc, :], kvall[2 * p + 1, vc, :]], axis=1)
            if opening:
                width = GROUP * DH
                q = q_ref[:, pl.ds(pl.multiple_of(g * width, T), width)]
                for r in range(GROUP):
                    qs[g, r * T : (r + 1) * T, :] = q[:, r * DH : (r + 1) * DH]
            for r in range(parts):
                at = slice(r * chunk, (r + 1) * chunk)
                s = dot(qs[g, at, :], keys)
                if opening:
                    shown = iota((chunk, chunk), 1) <= (iota((chunk, chunk), 0) % T) + b * T
                    s = jnp.where(shown, s, MASKED)
                peak = jnp.max(jnp.maximum(s[:, :T], s[:, T:]), axis=1, keepdims=True)
                if not opening:
                    old = top[g, at, :]
                    peak = jnp.maximum(old, peak)
                    shrink = jnp.exp2((old - peak) * EXP_SCALE)
                else:
                    peak = jnp.broadcast_to(peak, (chunk, T))
                top[g, at, :] = peak
                e0 = jnp.exp2((s[:, :T] - peak) * EXP_SCALE)
                e1 = jnp.exp2((s[:, T:] - peak) * EXP_SCALE)
                e = jnp.concatenate([e0.astype(BF), e1.astype(BF)], axis=1)
                summed = nt_dot(e, values)
                if opening:
                    total[g, at, :] = e0 + e1
                    acc[g, at, :] = summed
                else:
                    total[g, at, :] = total[g, at, :] * shrink + (e0 + e1)
                    acc[g, at, :] = acc[g, at, :] * shrink[:, :DH] + summed
            return 0

        lax.fori_loop(0, KVH, group, 0)

    def finish(g, _):
        width = GROUP * DH
        outs = []
        for r in range(GROUP):
            at = slice(r * T, (r + 1) * T)
            outs.append((acc[g, at, :] / jnp.sum(total[g, at, :], axis=1, keepdims=True)).astype(BF))
        att_ref[:, pl.ds(pl.multiple_of(g * width, T), width)] = jnp.concatenate(outs, axis=1)
        return 0

    chain_at = min(2, rows - 1)
    for d in range(rows):
        if d + 1 < rows:
            hand_on(d + 1)
        when = {0: a <= 1, chain_at: a > chain_at}.get(d, a == d + 1)
        if d <= chain_at:
            pl.when(when)(chain)

        @pl.when((b == 1) if d == 0 else (a - d >= 0))
        def _():
            kvarrive((a - d) * 2 + 1 - b)

        if d == 0:
            attend(a, True)
        else:
            @pl.when(a - d >= 0)
            def _():
                attend(a - d, False)

    lax.fori_loop(0, KVH, finish, 0)

    for c in range(CHUNKS):
        ecopy(c).wait_recv()
        for half in range(2):
            carried = dot(out_ref[...], ent[half, c])
            for e in range(CW // T):
                j = (half * CHUNKS + c) * (CW // T) + e
                factor = jnp.where(
                    left, ecum_ref[:, 2 * j : 2 * j + 1], ecum_ref[:, 2 * j + 1 : 2 * j + 2]
                )
                cols = slice(j * T, (j + 1) * T)
                mix_ref[:, cols] = (
                    inner[:, cols] + carried[:, e * T : (e + 1) * T] * factor
                ).astype(BF)

    fcopy().wait_send()
    for c in range(CHUNKS):
        ucopy(c).wait_send()
        ecopy(c).wait_send()

        @pl.when(a + 1 < rows)
        def _():
            scopy(c).wait_send()

    @pl.when(first)
    def _():
        kvside(0).wait_send()

    for d in range(rows):
        @pl.when((a - d >= 0) & (a + 1 < rows))
        def _():
            kvhop(d).wait_send()

        if d > 0:
            @pl.when(a - d >= 0)
            def _():
                kvside(d).wait_send()


def specs(count):
    return [pl.BlockSpec(memory_space=pltpu.VMEM)] * count


def per_device(n, mixer_input, input_map, output_map, log_decay, query_rows, key_rows, value_rows):
    width = MIXER_HEADS * P_SIZE
    rows = n // 2
    sem = pltpu.SemaphoreType.DMA
    chunked = pltpu.VMEM((CHUNKS, N, CW), BF)
    big = GROUP * T
    return pl.pallas_call(
        functools.partial(kernel, n),
        out_shape=(
            jax.ShapeDtypeStruct((T, width), BF),
            jax.ShapeDtypeStruct((T, QH * DH), BF),
        ),
        in_specs=specs(7),
        out_specs=specs(2),
        scratch_shapes=[
            pltpu.VMEM((n, KV_ROWS, T), BF),
            pltpu.VMEM((2, CHUNKS, N, CW), F32),
            pltpu.VMEM((2, 1, HALF), F32),
            pltpu.VMEM((T, width), F32),
            pltpu.VMEM((T, T), F32),
            chunked, chunked, pltpu.VMEM((1, HALF), F32), chunked, chunked, chunked,
            pltpu.VMEM((2, CHUNKS, N, CW), BF),
            pltpu.VMEM((KVH, big, DH), BF),
            pltpu.VMEM((KVH, big, T), F32),
            pltpu.VMEM((KVH, big, T), F32),
            pltpu.VMEM((KVH, big, DH), F32),
            sem((CHUNKS,)), sem((CHUNKS,)), sem((2,)), sem((CHUNKS,)), sem((CHUNKS,)),
            sem((CHUNKS,)), sem((CHUNKS,)), sem((rows,)), sem((n,)), sem((rows,)),
        ],
        compiler_params=pltpu.CompilerParams(
            collective_id=0, has_side_effects=True, vmem_limit_bytes=VMEM_LIMIT
        ),
        name="mix_and_attend",
    )(mixer_input, input_map, output_map, log_decay.T, query_rows, key_rows.T, value_rows.T)


def solution(mesh):
    rows = P(("dp", "ctx"), None)
    return jax.shard_map(
        functools.partial(per_device, mesh.shape["ctx"]),
        mesh=mesh,
        in_specs=(rows,) * 7,
        out_specs=(rows, rows),
        check_vma=False,
    )
```

```python
import functools
import math

import jax
import jax.numpy as jnp
from jax import lax
from jax.experimental import pallas as pl
from jax.experimental.pallas import tpu as pltpu
from jax.sharding import PartitionSpec as P

MIXER_HEADS = 40
P_SIZE = 64
N = 128
QH = 32
KVH = 4
DH = 80
T = 128
GROUP = QH // KVH
KV_ROWS = 2 * KVH * DH
CHUNKS = 5
CW = 256
PAIRS = MIXER_HEADS // 2
HALF = MIXER_HEADS * P_SIZE // 2
EXP_SCALE = math.log2(math.e) / math.sqrt(DH)
MASKED = -1e30
MESH = pl.DeviceIdType.MESH
BF = jnp.bfloat16
F32 = jnp.float32
VMEM_LIMIT = 56 * 1024 * 1024


def iota(shape, dim):
    return lax.broadcasted_iota(jnp.int32, shape, dim)


def nt_dot(a, b):
    return lax.dot_general(a, b, (((1,), (1,)), ((), ())), preferred_element_type=F32)


def dot(a, b):
    return jnp.dot(a, b, preferred_element_type=F32)


def kernel(
    n, x_ref, in_ref, out_ref, ld_ref, q_ref, k_ref, v_ref, mix_ref, att_ref,
    kvall, u, f, inner, ecum_ref, usend, urecv, frecv, sin, sout, entsend, ent,
    qs, top, total, acc,
    us_sem, ur_sem, f_sem, ss_sem, sr_sem, es_sem, er_sem, kvs_sem, kvr_sem, px_sem,
):
    dp = lax.axis_index("dp")
    me = lax.axis_index("ctx")
    a, b = me // 2, me % 2
    rows = n // 2
    partner = (dp, a * 2 + 1 - b)
    ahead = (dp, lax.rem(a + 1, rows) * 2 + b)
    behind = (dp, lax.rem(a + rows - 1, rows) * 2 + b)
    first = b == 0

    def ucopy(c):
        return pltpu.make_async_remote_copy(
            src_ref=usend.at[c], dst_ref=urecv.at[c], send_sem=us_sem.at[c],
            recv_sem=ur_sem.at[c], device_id=partner, device_id_type=MESH)

    def fcopy():
        return pltpu.make_async_remote_copy(
            src_ref=f.at[1 - b], dst_ref=frecv, send_sem=f_sem.at[0],
            recv_sem=f_sem.at[1], device_id=partner, device_id_type=MESH)

    def scopy(c):
        return pltpu.make_async_remote_copy(
            src_ref=sout.at[c], dst_ref=sin.at[c], send_sem=ss_sem.at[c],
            recv_sem=sr_sem.at[c], device_id=ahead, device_id_type=MESH)

    def ecopy(c):
        return pltpu.make_async_remote_copy(
            src_ref=entsend.at[c], dst_ref=ent.at[b, c], send_sem=es_sem.at[c],
            recv_sem=er_sem.at[c], device_id=partner, device_id_type=MESH)

    def kvhop(d):
        block = me - 2 * d
        return pltpu.make_async_remote_copy(
            src_ref=kvall.at[block], dst_ref=kvall.at[block], send_sem=kvs_sem.at[d],
            recv_sem=kvr_sem.at[block], device_id=ahead, device_id_type=MESH)

    def kvside(d):
        block = me - 2 * d
        return pltpu.make_async_remote_copy(
            src_ref=kvall.at[block], dst_ref=kvall.at[block], send_sem=px_sem.at[d],
            recv_sem=kvr_sem.at[block], device_id=partner, device_id_type=MESH)

    def kvarrive(block):
        pltpu.make_async_copy(kvall.at[block], kvall.at[block], kvr_sem.at[block]).wait()

    barrier = pltpu.get_barrier_semaphore()
    for device in (partner, ahead, behind):
        pl.semaphore_signal(barrier, inc=1, device_id=device, device_id_type=MESH)
    kvall[me, : KVH * DH, :] = k_ref[...]
    kvall[me, KVH * DH :, :] = v_ref[...]
    pl.semaphore_wait(barrier, 3)

    @pl.when(a + 1 < rows)
    def _():
        kvhop(0).start()

    lower = iota((T, T), 0) >= iota((T, T), 1)
    triu = jnp.where(iota((T, T), 0) <= iota((T, T), 1), 1.0, 0.0).astype(F32)
    cum_t = jnp.dot(ld_ref[...], triu, precision=lax.Precision.HIGHEST, preferred_element_type=F32)
    cum = jnp.concatenate([cum_t, jnp.zeros((T - MIXER_HEADS, T), F32)], axis=0).T
    ecum = jnp.exp(cum)
    ecum_ref[...] = ecum
    match = jnp.where(lower, nt_dot(out_ref[...], in_ref[...]), 0.0)
    in_t = in_ref[...].astype(F32).T
    left = iota((T, T), 1) < P_SIZE
    last = ecum[T - 1 : T, :]
    for j in range(PAIRS):
        half, place = divmod(j, PAIRS // 2)
        f[half, :, place * T : (place + 1) * T] = jnp.where(
            left[:1], last[:, 2 * j : 2 * j + 1], last[:, 2 * j + 1 : 2 * j + 2]
        )
    fcopy().start()
    for c in range(CHUNKS):
        for half in range(2):
            for e in range(CW // T):
                j = (half * CHUNKS + c) * (CW // T) + e
                stack = []
                tails = []
                for h in (2 * j, 2 * j + 1):
                    row = cum_t[h : h + 1, :]
                    gap = jnp.minimum(cum[:, h : h + 1] - row, 0.0)
                    stack.append((match * jnp.exp(gap)).astype(BF))
                    tails.append((in_t * jnp.exp(row[:, T - 1 :] - row)).astype(BF))
                cols = slice(j * T, (j + 1) * T)
                out = dot(jnp.concatenate(stack + tails, axis=0), x_ref[:, cols])
                inner[:, cols] = jnp.where(left, out[:T], out[T : 2 * T])
                u[half, c, :, e * T : (e + 1) * T] = jnp.where(
                    left, out[2 * T : 3 * T], out[3 * T :]
                )
        usend[c] = u[1 - b, c].astype(BF)
        ucopy(c).start()
        if c == 0:
            @pl.when(first)
            def _():
                kvside(0).start()

    @pl.when(first)
    def _():
        kvall[me + 1] = jnp.zeros((KV_ROWS, T), BF)

    def hand_on(d):
        @pl.when(a - d >= 0)
        def _():
            kvarrive(me - 2 * d)
            kvside(d).start()

            @pl.when(a + 1 < rows)
            def _():
                kvhop(d).start()

    def chain():
        fcopy().wait_recv()
        f_own = f[b]
        f_other = frecv[...]
        f_early = jnp.where(first, f_own, f_other)
        f_late = jnp.where(first, f_other, f_own)
        f_pair = f_early * f_late
        for c in range(CHUNKS):
            lanes = slice(c * CW, (c + 1) * CW)
            ucopy(c).wait_recv()
            u_own = u[b, c]
            u_other = urecv[c].astype(F32)
            early = jnp.where(first, u_own, u_other)
            late = jnp.where(first, u_other, u_own)
            pair = f_late[:, lanes] * early + late

            @pl.when(a == 0)
            def _():
                sin[c] = jnp.zeros((T, CW), BF)

            @pl.when(a > 0)
            def _():
                scopy(c).wait_recv()

            state = sin[c].astype(F32)

            @pl.when(a + 1 < rows)
            def _():
                sout[c] = (f_pair[:, lanes] * state + pair).astype(BF)
                scopy(c).start()

            middle = f_early[:, lanes] * state + early
            entsend[c] = jnp.where(first, middle, state).astype(BF)
            ecopy(c).start()
            ent[b, c] = jnp.where(first, state, middle).astype(BF)

    wide = 2 * T

    def attend(p, opening):
        def group(g, _):
            kc = pl.ds(pl.multiple_of(g * DH, 16), DH)
            vc = pl.ds(pl.multiple_of((KVH + g) * DH, 16), DH)
            keys = jnp.concatenate([kvall[2 * p, kc, :], kvall[2 * p + 1, kc, :]], axis=1)
            values = jnp.concatenate([kvall[2 * p, vc, :], kvall[2 * p + 1, vc, :]], axis=1)
            if opening:
                width = GROUP * DH
                q = q_ref[:, pl.ds(pl.multiple_of(g * width, T), width)]
                queries = jnp.concatenate([q[:, r * DH : (r + 1) * DH] for r in range(GROUP)], axis=0)
                qs[g] = queries
                shown = iota((T, wide), 1) <= iota((T, wide), 0) + b * T
            else:
                queries = qs[g]
                old_top = top[g]
                old_total = total[g]
                old_acc = acc[g]
            scores = dot(queries, keys)
            peaks, totals, shrinks, expos = [], [], [], []
            for r in range(GROUP):
                at = slice(r * T, (r + 1) * T)
                s = scores[at]
                if opening:
                    s = jnp.where(shown, s, MASKED)
                peak = jnp.max(jnp.maximum(s[:, :T], s[:, T:]), axis=1, keepdims=True)
                if opening:
                    peak = jnp.broadcast_to(peak, (T, T))
                else:
                    peak = jnp.maximum(old_top[at], peak)
                    shrinks.append(jnp.exp2((old_top[at] - peak) * EXP_SCALE))
                peaks.append(peak)
                e0 = jnp.exp2((s[:, :T] - peak) * EXP_SCALE)
                e1 = jnp.exp2((s[:, T:] - peak) * EXP_SCALE)
                totals.append(e0 + e1)
                expos.append(jnp.concatenate([e0.astype(BF), e1.astype(BF)], axis=1))
            summed = nt_dot(jnp.concatenate(expos, axis=0), values)
            for r in range(GROUP):
                at = slice(r * T, (r + 1) * T)
                top[g, at, :] = peaks[r]
                if opening:
                    total[g, at, :] = totals[r]
                    acc[g, at, :] = summed[at]
                else:
                    total[g, at, :] = old_total[at] * shrinks[r] + totals[r]
                    acc[g, at, :] = old_acc[at] * shrinks[r][:, :DH] + summed[at]
            return 0

        lax.fori_loop(0, KVH, group, 0)

    def finish(g, _):
        width = GROUP * DH
        outs = []
        for r in range(GROUP):
            at = slice(r * T, (r + 1) * T)
            outs.append((acc[g, at, :] / jnp.sum(total[g, at, :], axis=1, keepdims=True)).astype(BF))
        att_ref[:, pl.ds(pl.multiple_of(g * width, T), width)] = jnp.concatenate(outs, axis=1)
        return 0

    hand_on(1)

    @pl.when(a == 0)
    def _():
        chain()

    @pl.when(b == 1)
    def _():
        kvarrive(me - 1)

    attend(a, True)

    def step(d, _):
        hand_on(d + 1)

        @pl.when(a == d)
        def _():
            chain()

        kvarrive((a - d) * 2 + 1 - b)
        attend(a - d, False)
        return 0

    lax.fori_loop(1, a + 1, step, 0)
    lax.fori_loop(0, KVH, finish, 0)

    for c in range(CHUNKS):
        ecopy(c).wait_recv()
        for half in range(2):
            carried = dot(out_ref[...], ent[half, c])
            for e in range(CW // T):
                j = (half * CHUNKS + c) * (CW // T) + e
                factor = jnp.where(
                    left, ecum_ref[:, 2 * j : 2 * j + 1], ecum_ref[:, 2 * j + 1 : 2 * j + 2]
                )
                cols = slice(j * T, (j + 1) * T)
                mix_ref[:, cols] = (
                    inner[:, cols] + carried[:, e * T : (e + 1) * T] * factor
                ).astype(BF)

    fcopy().wait_send()
    for c in range(CHUNKS):
        ucopy(c).wait_send()
        ecopy(c).wait_send()

        @pl.when(a + 1 < rows)
        def _():
            scopy(c).wait_send()

    @pl.when(first)
    def _():
        kvside(0).wait_send()

    for d in range(rows):
        @pl.when((a - d >= 0) & (a + 1 < rows))
        def _():
            kvhop(d).wait_send()

        if d > 0:
            @pl.when(a - d >= 0)
            def _():
                kvside(d).wait_send()


def specs(count):
    return [pl.BlockSpec(memory_space=pltpu.VMEM)] * count


def per_device(n, mixer_input, input_map, output_map, log_decay, query_rows, key_rows, value_rows):
    width = MIXER_HEADS * P_SIZE
    rows = n // 2
    sem = pltpu.SemaphoreType.DMA
    chunked = pltpu.VMEM((CHUNKS, N, CW), BF)
    big = GROUP * T
    return pl.pallas_call(
        functools.partial(kernel, n),
        out_shape=(
            jax.ShapeDtypeStruct((T, width), BF),
            jax.ShapeDtypeStruct((T, QH * DH), BF),
        ),
        in_specs=specs(7),
        out_specs=specs(2),
        scratch_shapes=[
            pltpu.VMEM((n, KV_ROWS, T), BF),
            pltpu.VMEM((2, CHUNKS, N, CW), F32),
            pltpu.VMEM((2, 1, HALF), F32),
            pltpu.VMEM((T, width), F32),
            pltpu.VMEM((T, T), F32),
            chunked, chunked, pltpu.VMEM((1, HALF), F32), chunked, chunked, chunked,
            pltpu.VMEM((2, CHUNKS, N, CW), BF),
            pltpu.VMEM((KVH, big, DH), BF),
            pltpu.VMEM((KVH, big, T), F32),
            pltpu.VMEM((KVH, big, T), F32),
            pltpu.VMEM((KVH, big, DH), F32),
            sem((CHUNKS,)), sem((CHUNKS,)), sem((2,)), sem((CHUNKS,)), sem((CHUNKS,)),
            sem((CHUNKS,)), sem((CHUNKS,)), sem((rows,)), sem((n,)), sem((rows,)),
        ],
        compiler_params=pltpu.CompilerParams(
            collective_id=0, has_side_effects=True, vmem_limit_bytes=VMEM_LIMIT
        ),
        name="mix_and_attend",
    )(mixer_input, input_map, output_map, log_decay.T, query_rows, key_rows.T, value_rows.T)


def solution(mesh):
    rows = P(("dp", "ctx"), None)
    return jax.shard_map(
        functools.partial(per_device, mesh.shape["ctx"]),
        mesh=mesh,
        in_specs=(rows,) * 7,
        out_specs=(rows, rows),
        check_vma=False,
    )
```

```python
import functools
import math

import jax
import jax.numpy as jnp
from jax import lax
from jax.experimental import pallas as pl
from jax.experimental.pallas import tpu as pltpu
from jax.sharding import PartitionSpec as P

MIXER_HEADS = 40
P_SIZE = 64
N = 128
QH = 32
KVH = 4
DH = 80
T = 128
GROUP = QH // KVH
KV_ROWS = 2 * KVH * DH
CHUNKS = 5
CW = 256
PAIRS = MIXER_HEADS // 2
HALF = MIXER_HEADS * P_SIZE // 2
EXP_SCALE = math.log2(math.e) / math.sqrt(DH)
MASKED = -1e30
MESH = pl.DeviceIdType.MESH
BF = jnp.bfloat16
F32 = jnp.float32
VMEM_LIMIT = 56 * 1024 * 1024


def iota(shape, dim):
    return lax.broadcasted_iota(jnp.int32, shape, dim)


def nt_dot(a, b):
    return lax.dot_general(a, b, (((1,), (1,)), ((), ())), preferred_element_type=F32)


def dot(a, b):
    return jnp.dot(a, b, preferred_element_type=F32)


def kernel(
    n, x_ref, in_ref, out_ref, ld_ref, q_ref, k_ref, v_ref, mix_ref, att_ref,
    kvall, u, f, inner, ecum_ref, usend, urecv, frecv, sin, sout, entsend, ent,
    qs, top, total, acc,
    us_sem, ur_sem, f_sem, ss_sem, sr_sem, es_sem, er_sem, kvs_sem, kvr_sem, px_sem,
):
    dp = lax.axis_index("dp")
    me = lax.axis_index("ctx")
    a, b = me // 2, me % 2
    rows = n // 2
    partner = (dp, a * 2 + 1 - b)
    ahead = (dp, lax.rem(a + 1, rows) * 2 + b)
    behind = (dp, lax.rem(a + rows - 1, rows) * 2 + b)
    first = b == 0
    crossing = rows // 2
    early_pair = a < crossing
    more = a + 1 < rows

    def ucopy(c):
        return pltpu.make_async_remote_copy(
            src_ref=usend.at[c], dst_ref=urecv.at[c], send_sem=us_sem.at[c],
            recv_sem=ur_sem.at[c], device_id=partner, device_id_type=MESH)

    def fcopy():
        return pltpu.make_async_remote_copy(
            src_ref=f.at[1 - b], dst_ref=frecv, send_sem=f_sem.at[0],
            recv_sem=f_sem.at[1], device_id=partner, device_id_type=MESH)

    def scopy(c):
        return pltpu.make_async_remote_copy(
            src_ref=sout.at[c], dst_ref=sin.at[c], send_sem=ss_sem.at[c],
            recv_sem=sr_sem.at[c], device_id=ahead, device_id_type=MESH)

    def ecopy(c):
        return pltpu.make_async_remote_copy(
            src_ref=entsend.at[c], dst_ref=ent.at[b, c], send_sem=es_sem.at[c],
            recv_sem=er_sem.at[c], device_id=partner, device_id_type=MESH)

    def kvhop(d, e):
        block = (a - d) * 2 + e
        return pltpu.make_async_remote_copy(
            src_ref=kvall.at[block], dst_ref=kvall.at[block], send_sem=kvs_sem.at[d, e],
            recv_sem=kvr_sem.at[block], device_id=ahead, device_id_type=MESH)

    def kvside(d):
        block = me - 2 * d
        return pltpu.make_async_remote_copy(
            src_ref=kvall.at[block], dst_ref=kvall.at[block], send_sem=px_sem.at[d],
            recv_sem=kvr_sem.at[block], device_id=partner, device_id_type=MESH)

    def kvarrive(block):
        pltpu.make_async_copy(kvall.at[block], kvall.at[block], kvr_sem.at[block]).wait()

    barrier = pltpu.get_barrier_semaphore()
    for device in (partner, ahead, behind):
        pl.semaphore_signal(barrier, inc=1, device_id=device, device_id_type=MESH)
    kvall[me, : KVH * DH, :] = k_ref[...]
    kvall[me, KVH * DH :, :] = v_ref[...]
    pl.semaphore_wait(barrier, 3)

    @pl.when(more)
    def _():
        kvhop(0, b).start()

    lower = iota((T, T), 0) >= iota((T, T), 1)
    triu = jnp.where(iota((T, T), 0) <= iota((T, T), 1), 1.0, 0.0).astype(F32)
    cum_t = jnp.dot(ld_ref[...], triu, precision=lax.Precision.HIGHEST, preferred_element_type=F32)
    cum = jnp.concatenate([cum_t, jnp.zeros((T - MIXER_HEADS, T), F32)], axis=0).T
    ecum = jnp.exp(cum)
    ecum_ref[...] = ecum
    match = jnp.where(lower, nt_dot(out_ref[...], in_ref[...]), 0.0)
    in_t = in_ref[...].astype(F32).T
    left = iota((T, T), 1) < P_SIZE
    last = ecum[T - 1 : T, :]
    for j in range(PAIRS):
        half, place = divmod(j, PAIRS // 2)
        f[half, :, place * T : (place + 1) * T] = jnp.where(
            left[:1], last[:, 2 * j : 2 * j + 1], last[:, 2 * j + 1 : 2 * j + 2]
        )
    fcopy().start()
    for c in range(CHUNKS):
        for half in range(2):
            for e in range(CW // T):
                j = (half * CHUNKS + c) * (CW // T) + e
                stack = []
                tails = []
                for h in (2 * j, 2 * j + 1):
                    row = cum_t[h : h + 1, :]
                    gap = jnp.minimum(cum[:, h : h + 1] - row, 0.0)
                    stack.append((match * jnp.exp(gap)).astype(BF))
                    tails.append((in_t * jnp.exp(row[:, T - 1 :] - row)).astype(BF))
                cols = slice(j * T, (j + 1) * T)
                out = dot(jnp.concatenate(stack + tails, axis=0), x_ref[:, cols])
                inner[:, cols] = jnp.where(left, out[:T], out[T : 2 * T])
                u[half, c, :, e * T : (e + 1) * T] = jnp.where(
                    left, out[2 * T : 3 * T], out[3 * T :]
                )
        usend[c] = u[1 - b, c].astype(BF)
        ucopy(c).start()
        if c == 0:
            @pl.when(first | early_pair)
            def _():
                kvside(0).start()

    @pl.when(first & jnp.logical_not(early_pair))
    def _():
        kvall[me + 1] = jnp.zeros((KV_ROWS, T), BF)

    def hand_on(d):
        @pl.when(a - d >= crossing)
        def _():
            kvarrive(me - 2 * d)
            kvside(d).start()

            @pl.when(more)
            def _():
                kvhop(d, b).start()

        @pl.when((a - d >= 0) & (a - d < crossing))
        def _():
            for e in range(2):
                kvarrive((a - d) * 2 + e)

                @pl.when(more)
                def _():
                    kvhop(d, e).start()

    def chain():
        fcopy().wait_recv()
        f_own = f[b]
        f_other = frecv[...]
        f_early = jnp.where(first, f_own, f_other)
        f_late = jnp.where(first, f_other, f_own)
        f_pair = f_early * f_late
        for c in range(CHUNKS):
            lanes = slice(c * CW, (c + 1) * CW)
            ucopy(c).wait_recv()
            u_own = u[b, c]
            u_other = urecv[c].astype(F32)
            early = jnp.where(first, u_own, u_other)
            late = jnp.where(first, u_other, u_own)
            pair = f_late[:, lanes] * early + late

            @pl.when(a == 0)
            def _():
                sin[c] = jnp.zeros((T, CW), BF)

            @pl.when(a > 0)
            def _():
                scopy(c).wait_recv()

            state = sin[c].astype(F32)

            @pl.when(more)
            def _():
                sout[c] = (f_pair[:, lanes] * state + pair).astype(BF)
                scopy(c).start()

            middle = f_early[:, lanes] * state + early
            entsend[c] = jnp.where(first, middle, state).astype(BF)
            ecopy(c).start()
            ent[b, c] = jnp.where(first, state, middle).astype(BF)

    wide = 2 * T

    def attend(p, opening):
        def group(g, _):
            kc = pl.ds(pl.multiple_of(g * DH, 16), DH)
            vc = pl.ds(pl.multiple_of((KVH + g) * DH, 16), DH)
            keys = jnp.concatenate([kvall[2 * p, kc, :], kvall[2 * p + 1, kc, :]], axis=1)
            values = jnp.concatenate([kvall[2 * p, vc, :], kvall[2 * p + 1, vc, :]], axis=1)
            if opening:
                width = GROUP * DH
                q = q_ref[:, pl.ds(pl.multiple_of(g * width, T), width)]
                queries = jnp.concatenate([q[:, r * DH : (r + 1) * DH] for r in range(GROUP)], axis=0)
                qs[g] = queries
                shown = iota((T, wide), 1) <= iota((T, wide), 0) + b * T
            else:
                queries = qs[g]
                old_top = top[g]
                old_total = total[g]
                old_acc = acc[g]
            scores = dot(queries, keys)
            peaks, totals, shrinks, expos = [], [], [], []
            for r in range(GROUP):
                at = slice(r * T, (r + 1) * T)
                s = scores[at]
                if opening:
                    s = jnp.where(shown, s, MASKED)
                peak = jnp.max(jnp.maximum(s[:, :T], s[:, T:]), axis=1, keepdims=True)
                if opening:
                    peak = jnp.broadcast_to(peak, (T, T))
                else:
                    peak = jnp.maximum(old_top[at], peak)
                    shrinks.append(jnp.exp2((old_top[at] - peak) * EXP_SCALE))
                peaks.append(peak)
                e0 = jnp.exp2((s[:, :T] - peak) * EXP_SCALE)
                e1 = jnp.exp2((s[:, T:] - peak) * EXP_SCALE)
                totals.append(e0 + e1)
                expos.append(jnp.concatenate([e0.astype(BF), e1.astype(BF)], axis=1))
            summed = nt_dot(jnp.concatenate(expos, axis=0), values)
            for r in range(GROUP):
                at = slice(r * T, (r + 1) * T)
                top[g, at, :] = peaks[r]
                if opening:
                    total[g, at, :] = totals[r]
                    acc[g, at, :] = summed[at]
                else:
                    total[g, at, :] = old_total[at] * shrinks[r] + totals[r]
                    acc[g, at, :] = old_acc[at] * shrinks[r][:, :DH] + summed[at]
            return 0

        lax.fori_loop(0, KVH, group, 0)

    def finish(g, _):
        width = GROUP * DH
        outs = []
        for r in range(GROUP):
            at = slice(r * T, (r + 1) * T)
            outs.append((acc[g, at, :] / jnp.sum(total[g, at, :], axis=1, keepdims=True)).astype(BF))
        att_ref[:, pl.ds(pl.multiple_of(g * width, T), width)] = jnp.concatenate(outs, axis=1)
        return 0

    hand_on(1)

    @pl.when(a == 0)
    def _():
        chain()

    @pl.when((b == 1) | early_pair)
    def _():
        kvarrive(a * 2 + 1 - b)

    @pl.when(early_pair)
    def _():
        kvhop(0, 1 - b).start()

    attend(a, True)

    def step(d, _):
        hand_on(d + 1)

        @pl.when(a == d)
        def _():
            chain()


        @pl.when(a - d >= crossing)
        def _():
            kvarrive((a - d) * 2 + 1 - b)

        attend(a - d, False)
        return 0

    lax.fori_loop(1, a + 1, step, 0)
    lax.fori_loop(0, KVH, finish, 0)

    for c in range(CHUNKS):
        ecopy(c).wait_recv()
        for half in range(2):
            carried = dot(out_ref[...], ent[half, c])
            for e in range(CW // T):
                j = (half * CHUNKS + c) * (CW // T) + e
                factor = jnp.where(
                    left, ecum_ref[:, 2 * j : 2 * j + 1], ecum_ref[:, 2 * j + 1 : 2 * j + 2]
                )
                cols = slice(j * T, (j + 1) * T)
                mix_ref[:, cols] = (
                    inner[:, cols] + carried[:, e * T : (e + 1) * T] * factor
                ).astype(BF)

    fcopy().wait_send()
    for c in range(CHUNKS):
        ucopy(c).wait_send()
        ecopy(c).wait_send()

        @pl.when(more)
        def _():
            scopy(c).wait_send()

    @pl.when(first | early_pair)
    def _():
        kvside(0).wait_send()

    @pl.when(more)
    def _():
        kvhop(0, b).wait_send()

    @pl.when(early_pair)
    def _():
        kvhop(0, 1 - b).wait_send()

    def settle(d, _):
        @pl.when(a - d >= crossing)
        def _():
            kvside(d).wait_send()

            @pl.when(more)
            def _():
                kvhop(d, b).wait_send()

        @pl.when((a - d < crossing) & more)
        def _():
            for e in range(2):
                kvhop(d, e).wait_send()

        return 0

    lax.fori_loop(1, a + 1, settle, 0)


def specs(count):
    return [pl.BlockSpec(memory_space=pltpu.VMEM)] * count


def per_device(n, mixer_input, input_map, output_map, log_decay, query_rows, key_rows, value_rows):
    width = MIXER_HEADS * P_SIZE
    rows = n // 2
    sem = pltpu.SemaphoreType.DMA
    chunked = pltpu.VMEM((CHUNKS, N, CW), BF)
    big = GROUP * T
    return pl.pallas_call(
        functools.partial(kernel, n),
        out_shape=(
            jax.ShapeDtypeStruct((T, width), BF),
            jax.ShapeDtypeStruct((T, QH * DH), BF),
        ),
        in_specs=specs(7),
        out_specs=specs(2),
        scratch_shapes=[
            pltpu.VMEM((n, KV_ROWS, T), BF),
            pltpu.VMEM((2, CHUNKS, N, CW), F32),
            pltpu.VMEM((2, 1, HALF), F32),
            pltpu.VMEM((T, width), F32),
            pltpu.VMEM((T, T), F32),
            chunked, chunked, pltpu.VMEM((1, HALF), F32), chunked, chunked, chunked,
            pltpu.VMEM((2, CHUNKS, N, CW), BF),
            pltpu.VMEM((KVH, big, DH), BF),
            pltpu.VMEM((KVH, big, T), F32),
            pltpu.VMEM((KVH, big, T), F32),
            pltpu.VMEM((KVH, big, DH), F32),
            sem((CHUNKS,)), sem((CHUNKS,)), sem((2,)), sem((CHUNKS,)), sem((CHUNKS,)),
            sem((CHUNKS,)), sem((CHUNKS,)), sem((rows, 2)), sem((n,)), sem((rows,)),
        ],
        compiler_params=pltpu.CompilerParams(
            collective_id=0, has_side_effects=True, vmem_limit_bytes=VMEM_LIMIT
        ),
        name="mix_and_attend",
    )(mixer_input, input_map, output_map, log_decay.T, query_rows, key_rows.T, value_rows.T)


def solution(mesh):
    rows = P(("dp", "ctx"), None)
    return jax.shard_map(
        functools.partial(per_device, mesh.shape["ctx"]),
        mesh=mesh,
        in_specs=(rows,) * 7,
        out_specs=(rows, rows),
        check_vma=False,
    )
```

```python
import functools
import math

import jax
import jax.numpy as jnp
from jax import lax
from jax.experimental import pallas as pl
from jax.experimental.pallas import tpu as pltpu
from jax.sharding import PartitionSpec as P

MIXER_HEADS = 40
P_SIZE = 64
N = 128
QH = 32
KVH = 4
DH = 80
T = 128
GROUP = QH // KVH
KV_ROWS = 2 * KVH * DH
CHUNKS = 5
CW = 256
PAIRS = MIXER_HEADS // 2
HALF = MIXER_HEADS * P_SIZE // 2
EXP_SCALE = math.log2(math.e) / math.sqrt(DH)
MASKED = -1e30
MESH = pl.DeviceIdType.MESH
BF = jnp.bfloat16
F32 = jnp.float32
VMEM_LIMIT = 56 * 1024 * 1024


def iota(shape, dim):
    return lax.broadcasted_iota(jnp.int32, shape, dim)


def nt_dot(a, b):
    return lax.dot_general(a, b, (((1,), (1,)), ((), ())), preferred_element_type=F32)


def dot(a, b):
    return jnp.dot(a, b, preferred_element_type=F32)


def kernel(
    n, x_ref, in_ref, out_ref, ld_ref, q_ref, k_ref, v_ref, mix_ref, att_ref,
    kvall, u, f, inner, ecum_ref, usend, urecv, frecv, sin, sout, entsend, ent,
    qs, top, total, acc,
    us_sem, ur_sem, f_sem, ss_sem, sr_sem, es_sem, er_sem, kvs_sem, kvr_sem, px_sem,
):
    dp = lax.axis_index("dp")
    me = lax.axis_index("ctx")
    a, b = me // 2, me % 2
    rows = n // 2
    partner = (dp, a * 2 + 1 - b)
    ahead = (dp, lax.rem(a + 1, rows) * 2 + b)
    behind = (dp, lax.rem(a + rows - 1, rows) * 2 + b)
    first = b == 0
    crossing = max(1, rows // 4)
    early_pair = a < crossing
    more = a + 1 < rows

    def ucopy(c):
        return pltpu.make_async_remote_copy(
            src_ref=usend.at[c], dst_ref=urecv.at[c], send_sem=us_sem.at[c],
            recv_sem=ur_sem.at[c], device_id=partner, device_id_type=MESH)

    def fcopy():
        return pltpu.make_async_remote_copy(
            src_ref=f.at[1 - b], dst_ref=frecv, send_sem=f_sem.at[0],
            recv_sem=f_sem.at[1], device_id=partner, device_id_type=MESH)

    def scopy(c):
        return pltpu.make_async_remote_copy(
            src_ref=sout.at[c], dst_ref=sin.at[c], send_sem=ss_sem.at[c],
            recv_sem=sr_sem.at[c], device_id=ahead, device_id_type=MESH)

    def ecopy(c):
        return pltpu.make_async_remote_copy(
            src_ref=entsend.at[c], dst_ref=ent.at[b, c], send_sem=es_sem.at[c],
            recv_sem=er_sem.at[c], device_id=partner, device_id_type=MESH)

    def kvhop(d, e):
        block = (a - d) * 2 + e
        return pltpu.make_async_remote_copy(
            src_ref=kvall.at[block], dst_ref=kvall.at[block], send_sem=kvs_sem.at[d, e],
            recv_sem=kvr_sem.at[block], device_id=ahead, device_id_type=MESH)

    def kvside(d):
        block = me - 2 * d
        return pltpu.make_async_remote_copy(
            src_ref=kvall.at[block], dst_ref=kvall.at[block], send_sem=px_sem.at[d],
            recv_sem=kvr_sem.at[block], device_id=partner, device_id_type=MESH)

    def kvarrive(block):
        pltpu.make_async_copy(kvall.at[block], kvall.at[block], kvr_sem.at[block]).wait()

    barrier = pltpu.get_barrier_semaphore()
    for device in (partner, ahead, behind):
        pl.semaphore_signal(barrier, inc=1, device_id=device, device_id_type=MESH)
    kvall[me, : KVH * DH, :] = k_ref[...]
    kvall[me, KVH * DH :, :] = v_ref[...]
    pl.semaphore_wait(barrier, 3)

    @pl.when(more)
    def _():
        kvhop(0, b).start()

    @pl.when(first | early_pair)
    def _():
        kvside(0).start()

    lower = iota((T, T), 0) >= iota((T, T), 1)
    triu = jnp.where(iota((T, T), 0) <= iota((T, T), 1), 1.0, 0.0).astype(F32)
    cum_t = jnp.dot(ld_ref[...], triu, precision=lax.Precision.HIGHEST, preferred_element_type=F32)
    cum = jnp.concatenate([cum_t, jnp.zeros((T - MIXER_HEADS, T), F32)], axis=0).T
    ecum = jnp.exp(cum)
    ecum_ref[...] = ecum
    match = jnp.where(lower, nt_dot(out_ref[...], in_ref[...]), 0.0)
    in_t = in_ref[...].astype(F32).T
    left = iota((T, T), 1) < P_SIZE
    last = ecum[T - 1 : T, :]
    for j in range(PAIRS):
        half, place = divmod(j, PAIRS // 2)
        f[half, :, place * T : (place + 1) * T] = jnp.where(
            left[:1], last[:, 2 * j : 2 * j + 1], last[:, 2 * j + 1 : 2 * j + 2]
        )
    fcopy().start()
    for c in range(CHUNKS):
        for half in range(2):
            for e in range(CW // T):
                j = (half * CHUNKS + c) * (CW // T) + e
                stack = []
                tails = []
                for h in (2 * j, 2 * j + 1):
                    row = cum_t[h : h + 1, :]
                    gap = jnp.minimum(cum[:, h : h + 1] - row, 0.0)
                    stack.append((match * jnp.exp(gap)).astype(BF))
                    tails.append((in_t * jnp.exp(row[:, T - 1 :] - row)).astype(BF))
                cols = slice(j * T, (j + 1) * T)
                out = dot(jnp.concatenate(stack + tails, axis=0), x_ref[:, cols])
                inner[:, cols] = jnp.where(left, out[:T], out[T : 2 * T])
                u[half, c, :, e * T : (e + 1) * T] = jnp.where(
                    left, out[2 * T : 3 * T], out[3 * T :]
                )
        usend[c] = u[1 - b, c].astype(BF)
        ucopy(c).start()

    @pl.when(first & jnp.logical_not(early_pair))
    def _():
        kvall[me + 1] = jnp.zeros((KV_ROWS, T), BF)

    def hand_on(d):
        @pl.when(a - d >= 0)
        def _():
            kvarrive(me - 2 * d)

            @pl.when(more)
            def _():
                kvhop(d, b).start()

        @pl.when(a - d >= crossing)
        def _():
            kvside(d).start()

    def hand_other(d):
        kvarrive((a - d) * 2 + 1 - b)

        @pl.when((a - d < crossing) & more)
        def _():
            kvhop(d, 1 - b).start()

    def chain():
        fcopy().wait_recv()
        f_own = f[b]
        f_other = frecv[...]
        f_early = jnp.where(first, f_own, f_other)
        f_late = jnp.where(first, f_other, f_own)
        f_pair = f_early * f_late
        for c in range(CHUNKS):
            lanes = slice(c * CW, (c + 1) * CW)
            ucopy(c).wait_recv()
            u_own = u[b, c]
            u_other = urecv[c].astype(F32)
            early = jnp.where(first, u_own, u_other)
            late = jnp.where(first, u_other, u_own)
            pair = f_late[:, lanes] * early + late

            @pl.when(a == 0)
            def _():
                sin[c] = jnp.zeros((T, CW), BF)

            @pl.when(a > 0)
            def _():
                scopy(c).wait_recv()

            state = sin[c].astype(F32)

            @pl.when(more)
            def _():
                sout[c] = (f_pair[:, lanes] * state + pair).astype(BF)
                scopy(c).start()

            middle = f_early[:, lanes] * state + early
            entsend[c] = jnp.where(first, middle, state).astype(BF)
            ecopy(c).start()
            ent[b, c] = jnp.where(first, state, middle).astype(BF)

    wide = 2 * T

    def attend(p, opening):
        def group(g, _):
            kc = pl.ds(pl.multiple_of(g * DH, 16), DH)
            vc = pl.ds(pl.multiple_of((KVH + g) * DH, 16), DH)
            keys = jnp.concatenate([kvall[2 * p, kc, :], kvall[2 * p + 1, kc, :]], axis=1)
            values = jnp.concatenate([kvall[2 * p, vc, :], kvall[2 * p + 1, vc, :]], axis=1)
            if opening:
                width = GROUP * DH
                q = q_ref[:, pl.ds(pl.multiple_of(g * width, T), width)]
                queries = jnp.concatenate([q[:, r * DH : (r + 1) * DH] for r in range(GROUP)], axis=0)
                qs[g] = queries
                shown = iota((T, wide), 1) <= iota((T, wide), 0) + b * T
            else:
                queries = qs[g]
                old_top = top[g]
                old_total = total[g]
                old_acc = acc[g]
            scores = dot(queries, keys)
            peaks, totals, shrinks, expos = [], [], [], []
            for r in range(GROUP):
                at = slice(r * T, (r + 1) * T)
                s = scores[at]
                if opening:
                    s = jnp.where(shown, s, MASKED)
                peak = jnp.max(jnp.maximum(s[:, :T], s[:, T:]), axis=1, keepdims=True)
                if opening:
                    peak = jnp.broadcast_to(peak, (T, T))
                else:
                    peak = jnp.maximum(old_top[at], peak)
                    shrinks.append(jnp.exp2((old_top[at] - peak) * EXP_SCALE))
                peaks.append(peak)
                e0 = jnp.exp2((s[:, :T] - peak) * EXP_SCALE)
                e1 = jnp.exp2((s[:, T:] - peak) * EXP_SCALE)
                totals.append(e0 + e1)
                expos.append(jnp.concatenate([e0.astype(BF), e1.astype(BF)], axis=1))
            summed = nt_dot(jnp.concatenate(expos, axis=0), values)
            for r in range(GROUP):
                at = slice(r * T, (r + 1) * T)
                top[g, at, :] = peaks[r]
                if opening:
                    total[g, at, :] = totals[r]
                    acc[g, at, :] = summed[at]
                else:
                    total[g, at, :] = old_total[at] * shrinks[r] + totals[r]
                    acc[g, at, :] = old_acc[at] * shrinks[r][:, :DH] + summed[at]
            return 0

        lax.fori_loop(0, KVH, group, 0)

    def finish(g, _):
        width = GROUP * DH
        outs = []
        for r in range(GROUP):
            at = slice(r * T, (r + 1) * T)
            outs.append((acc[g, at, :] / jnp.sum(total[g, at, :], axis=1, keepdims=True)).astype(BF))
        att_ref[:, pl.ds(pl.multiple_of(g * width, T), width)] = jnp.concatenate(outs, axis=1)
        return 0

    hand_on(1)

    @pl.when((b == 1) | early_pair)
    def _():
        hand_other(0)

    @pl.when(a == 0)
    def _():
        chain()

    attend(a, True)

    def step(d, _):
        hand_on(d + 1)
        hand_other(d)

        @pl.when(a == d)
        def _():
            chain()

        attend(a - d, False)
        return 0

    lax.fori_loop(1, a + 1, step, 0)
    lax.fori_loop(0, KVH, finish, 0)

    for c in range(CHUNKS):
        ecopy(c).wait_recv()
        for half in range(2):
            carried = dot(out_ref[...], ent[half, c])
            for e in range(CW // T):
                j = (half * CHUNKS + c) * (CW // T) + e
                factor = jnp.where(
                    left, ecum_ref[:, 2 * j : 2 * j + 1], ecum_ref[:, 2 * j + 1 : 2 * j + 2]
                )
                cols = slice(j * T, (j + 1) * T)
                mix_ref[:, cols] = (
                    inner[:, cols] + carried[:, e * T : (e + 1) * T] * factor
                ).astype(BF)

    fcopy().wait_send()
    for c in range(CHUNKS):
        ucopy(c).wait_send()
        ecopy(c).wait_send()

        @pl.when(more)
        def _():
            scopy(c).wait_send()

    @pl.when(first | early_pair)
    def _():
        kvside(0).wait_send()

    def settle(d, _):
        @pl.when((a - d >= crossing) & (d > 0))
        def _():
            kvside(d).wait_send()

        @pl.when(more)
        def _():
            kvhop(d, b).wait_send()

        @pl.when((a - d < crossing) & more)
        def _():
            kvhop(d, 1 - b).wait_send()

        return 0

    lax.fori_loop(0, a + 1, settle, 0)


def specs(count):
    return [pl.BlockSpec(memory_space=pltpu.VMEM)] * count


def per_device(n, mixer_input, input_map, output_map, log_decay, query_rows, key_rows, value_rows):
    width = MIXER_HEADS * P_SIZE
    rows = n // 2
    sem = pltpu.SemaphoreType.DMA
    chunked = pltpu.VMEM((CHUNKS, N, CW), BF)
    big = GROUP * T
    return pl.pallas_call(
        functools.partial(kernel, n),
        out_shape=(
            jax.ShapeDtypeStruct((T, width), BF),
            jax.ShapeDtypeStruct((T, QH * DH), BF),
        ),
        in_specs=specs(7),
        out_specs=specs(2),
        scratch_shapes=[
            pltpu.VMEM((n, KV_ROWS, T), BF),
            pltpu.VMEM((2, CHUNKS, N, CW), F32),
            pltpu.VMEM((2, 1, HALF), F32),
            pltpu.VMEM((T, width), F32),
            pltpu.VMEM((T, T), F32),
            chunked, chunked, pltpu.VMEM((1, HALF), F32), chunked, chunked, chunked,
            pltpu.VMEM((2, CHUNKS, N, CW), BF),
            pltpu.VMEM((KVH, big, DH), BF),
            pltpu.VMEM((KVH, big, T), F32),
            pltpu.VMEM((KVH, big, T), F32),
            pltpu.VMEM((KVH, big, DH), F32),
            sem((CHUNKS,)), sem((CHUNKS,)), sem((2,)), sem((CHUNKS,)), sem((CHUNKS,)),
            sem((CHUNKS,)), sem((CHUNKS,)), sem((rows, 2)), sem((n,)), sem((rows,)),
        ],
        compiler_params=pltpu.CompilerParams(
            collective_id=0, has_side_effects=True, vmem_limit_bytes=VMEM_LIMIT
        ),
        name="mix_and_attend",
    )(mixer_input, input_map, output_map, log_decay.T, query_rows, key_rows.T, value_rows.T)


def solution(mesh):
    rows = P(("dp", "ctx"), None)
    return jax.shard_map(
        functools.partial(per_device, mesh.shape["ctx"]),
        mesh=mesh,
        in_specs=(rows,) * 7,
        out_specs=(rows, rows),
        check_vma=False,
    )
```

```python
import functools
import math

import jax
import jax.numpy as jnp
from jax import lax
from jax.experimental import pallas as pl
from jax.experimental.pallas import tpu as pltpu
from jax.sharding import PartitionSpec as P

MIXER_HEADS = 40
P_SIZE = 64
N = 128
QH = 32
KVH = 4
DH = 80
T = 128
GROUP = QH // KVH
KV_ROWS = 2 * KVH * DH
CHUNKS = 5
CW = 256
PAIRS = MIXER_HEADS // 2
HALF = MIXER_HEADS * P_SIZE // 2
EXP_SCALE = math.log2(math.e) / math.sqrt(DH)
MASKED = -1e30
MESH = pl.DeviceIdType.MESH
BF = jnp.bfloat16
F32 = jnp.float32
VMEM_LIMIT = 56 * 1024 * 1024


def iota(shape, dim):
    return lax.broadcasted_iota(jnp.int32, shape, dim)


def nt_dot(a, b):
    return lax.dot_general(a, b, (((1,), (1,)), ((), ())), preferred_element_type=F32)


def dot(a, b):
    return jnp.dot(a, b, preferred_element_type=F32)


def kernel(
    n, x_ref, in_ref, out_ref, ld_ref, q_ref, k_ref, v_ref, mix_ref, att_ref,
    kvall, u, f, inner, ecum_ref, usend, urecv, frecv, sin, sout, entsend, ent,
    qs, top, total, acc,
    us_sem, ur_sem, f_sem, ss_sem, sr_sem, es_sem, er_sem, kvs_sem, kvr_sem, px_sem,
):
    dp = lax.axis_index("dp")
    me = lax.axis_index("ctx")
    a, b = me // 2, me % 2
    rows = n // 2
    partner = (dp, a * 2 + 1 - b)
    ahead = (dp, lax.rem(a + 1, rows) * 2 + b)
    behind = (dp, lax.rem(a + rows - 1, rows) * 2 + b)
    first = b == 0

    def ucopy(c):
        return pltpu.make_async_remote_copy(
            src_ref=usend.at[c], dst_ref=urecv.at[c], send_sem=us_sem.at[c],
            recv_sem=ur_sem.at[c], device_id=partner, device_id_type=MESH)

    def fcopy():
        return pltpu.make_async_remote_copy(
            src_ref=f.at[1 - b], dst_ref=frecv, send_sem=f_sem.at[0],
            recv_sem=f_sem.at[1], device_id=partner, device_id_type=MESH)

    def scopy(c):
        return pltpu.make_async_remote_copy(
            src_ref=sout.at[c], dst_ref=sin.at[c], send_sem=ss_sem.at[c],
            recv_sem=sr_sem.at[c], device_id=ahead, device_id_type=MESH)

    def ecopy(c):
        return pltpu.make_async_remote_copy(
            src_ref=entsend.at[c], dst_ref=ent.at[b, c], send_sem=es_sem.at[c],
            recv_sem=er_sem.at[c], device_id=partner, device_id_type=MESH)

    def kvhop(d):
        block = me - 2 * d
        return pltpu.make_async_remote_copy(
            src_ref=kvall.at[block], dst_ref=kvall.at[block], send_sem=kvs_sem.at[d],
            recv_sem=kvr_sem.at[block], device_id=ahead, device_id_type=MESH)

    def kvside(d):
        block = me - 2 * d
        return pltpu.make_async_remote_copy(
            src_ref=kvall.at[block], dst_ref=kvall.at[block], send_sem=px_sem.at[d],
            recv_sem=kvr_sem.at[block], device_id=partner, device_id_type=MESH)

    def kvarrive(block):
        pltpu.make_async_copy(kvall.at[block], kvall.at[block], kvr_sem.at[block]).wait()

    barrier = pltpu.get_barrier_semaphore()
    for device in (partner, ahead, behind):
        pl.semaphore_signal(barrier, inc=1, device_id=device, device_id_type=MESH)
    kvall[me, : KVH * DH, :] = k_ref[...]
    kvall[me, KVH * DH :, :] = v_ref[...]
    pl.semaphore_wait(barrier, 3)

    @pl.when(a + 1 < rows)
    def _():
        kvhop(0).start()

    lower = iota((T, T), 0) >= iota((T, T), 1)
    triu = jnp.where(iota((T, T), 0) <= iota((T, T), 1), 1.0, 0.0).astype(F32)
    cum_t = jnp.dot(ld_ref[...], triu, precision=lax.Precision.HIGHEST, preferred_element_type=F32)
    cum = jnp.concatenate([cum_t, jnp.zeros((T - MIXER_HEADS, T), F32)], axis=0).T
    ecum = jnp.exp(cum)
    ecum_ref[...] = ecum
    match = jnp.where(lower, nt_dot(out_ref[...], in_ref[...]), 0.0)
    in_t = in_ref[...].astype(F32).T
    left = iota((T, T), 1) < P_SIZE
    last = ecum[T - 1 : T, :]
    for j in range(PAIRS):
        half, place = divmod(j, PAIRS // 2)
        f[half, :, place * T : (place + 1) * T] = jnp.where(
            left[:1], last[:, 2 * j : 2 * j + 1], last[:, 2 * j + 1 : 2 * j + 2]
        )
    fcopy().start()
    for c in range(CHUNKS):
        for half in range(2):
            for e in range(CW // T):
                j = (half * CHUNKS + c) * (CW // T) + e
                stack = []
                tails = []
                for h in (2 * j, 2 * j + 1):
                    row = cum_t[h : h + 1, :]
                    gap = jnp.minimum(cum[:, h : h + 1] - row, 0.0)
                    stack.append((match * jnp.exp(gap)).astype(BF))
                    tails.append((in_t * jnp.exp(row[:, T - 1 :] - row)).astype(BF))
                cols = slice(j * T, (j + 1) * T)
                out = dot(jnp.concatenate(stack + tails, axis=0), x_ref[:, cols])
                inner[:, cols] = jnp.where(left, out[:T], out[T : 2 * T])
                u[half, c, :, e * T : (e + 1) * T] = jnp.where(
                    left, out[2 * T : 3 * T], out[3 * T :]
                )
        usend[c] = u[1 - b, c].astype(BF)
        ucopy(c).start()
        if c == 0:
            @pl.when(first)
            def _():
                kvside(0).start()

    @pl.when(first)
    def _():
        kvall[me + 1] = jnp.zeros((KV_ROWS, T), BF)

    def hand_on(d):
        @pl.when(a - d >= 0)
        def _():
            kvarrive(me - 2 * d)
            kvside(d).start()

            @pl.when(a + 1 < rows)
            def _():
                kvhop(d).start()

    def chain():
        fcopy().wait_recv()
        f_own = f[b]
        f_other = frecv[...]
        f_early = jnp.where(first, f_own, f_other)
        f_late = jnp.where(first, f_other, f_own)
        f_pair = f_early * f_late
        for c in range(CHUNKS):
            lanes = slice(c * CW, (c + 1) * CW)
            ucopy(c).wait_recv()
            u_own = u[b, c]
            u_other = urecv[c].astype(F32)
            early = jnp.where(first, u_own, u_other)
            late = jnp.where(first, u_other, u_own)
            pair = f_late[:, lanes] * early + late

            @pl.when(a == 0)
            def _():
                sin[c] = jnp.zeros((T, CW), BF)

            @pl.when(a > 0)
            def _():
                scopy(c).wait_recv()

            state = sin[c].astype(F32)

            @pl.when(a + 1 < rows)
            def _():
                sout[c] = (f_pair[:, lanes] * state + pair).astype(BF)
                scopy(c).start()

            middle = f_early[:, lanes] * state + early
            entsend[c] = jnp.where(first, middle, state).astype(BF)
            ecopy(c).start()
            ent[b, c] = jnp.where(first, state, middle).astype(BF)

    wide = 2 * T

    def attend(p, opening):
        def group(g, _):
            kc = pl.ds(pl.multiple_of(g * DH, 16), DH)
            vc = pl.ds(pl.multiple_of((KVH + g) * DH, 16), DH)
            keys = jnp.concatenate([kvall[2 * p, kc, :], kvall[2 * p + 1, kc, :]], axis=1).T
            values = jnp.concatenate([kvall[2 * p, vc, :], kvall[2 * p + 1, vc, :]], axis=1)
            if opening:
                q = q_ref[:, pl.ds(pl.multiple_of(g * GROUP * DH, T), GROUP * DH)].T
                queries = jnp.concatenate([q[r * DH : (r + 1) * DH] for r in range(GROUP)], axis=1)
                qs[g] = queries
                shown = iota((wide, wide), 0) <= (iota((wide, wide), 1) % T) + b * T
            else:
                queries = qs[g]
                old_top = top[g]
                old_total = total[g]
                old_acc = acc[g]
            results = []
            for r in range(GROUP // 2):
                at = slice(r * wide, (r + 1) * wide)
                s = dot(keys, queries[:, at])
                if opening:
                    s = jnp.where(shown, s, MASKED)
                peak = jnp.max(s, axis=0, keepdims=True)
                if not opening:
                    peak = jnp.maximum(old_top[:, at], peak)
                e = jnp.exp2((s - peak) * EXP_SCALE)
                summed = jnp.sum(e, axis=0, keepdims=True)
                out = dot(values, e.astype(BF))
                if not opening:
                    shrink = jnp.exp2((old_top[:, at] - peak) * EXP_SCALE)
                    summed = old_total[:, at] * shrink + summed
                    out = old_acc[:, at] * shrink + out
                results.append((peak, summed, out))
            for r in range(GROUP // 2):
                at = slice(r * wide, (r + 1) * wide)
                top[g, :, at], total[g, :, at], acc[g, :, at] = results[r]
            return 0

        lax.fori_loop(0, KVH, group, 0)

    def finish(g, _):
        out = acc[g] / total[g]
        tall = jnp.concatenate([out[:, r * T : (r + 1) * T] for r in range(GROUP)], axis=0)
        att_ref[:, pl.ds(pl.multiple_of(g * GROUP * DH, T), GROUP * DH)] = tall.T.astype(BF)
        return 0

    hand_on(1)

    @pl.when(a == 0)
    def _():
        chain()

    @pl.when(b == 1)
    def _():
        kvarrive(me - 1)

    attend(a, True)

    def step(d, _):
        hand_on(d + 1)

        @pl.when(a == d)
        def _():
            chain()

        kvarrive((a - d) * 2 + 1 - b)
        attend(a - d, False)
        return 0

    lax.fori_loop(1, a + 1, step, 0)
    lax.fori_loop(0, KVH, finish, 0)

    for c in range(CHUNKS):
        ecopy(c).wait_recv()
        for half in range(2):
            carried = dot(out_ref[...], ent[half, c])
            for e in range(CW // T):
                j = (half * CHUNKS + c) * (CW // T) + e
                factor = jnp.where(
                    left, ecum_ref[:, 2 * j : 2 * j + 1], ecum_ref[:, 2 * j + 1 : 2 * j + 2]
                )
                cols = slice(j * T, (j + 1) * T)
                mix_ref[:, cols] = (
                    inner[:, cols] + carried[:, e * T : (e + 1) * T] * factor
                ).astype(BF)

    fcopy().wait_send()
    for c in range(CHUNKS):
        ucopy(c).wait_send()
        ecopy(c).wait_send()

        @pl.when(a + 1 < rows)
        def _():
            scopy(c).wait_send()

    @pl.when(first)
    def _():
        kvside(0).wait_send()

    for d in range(rows):
        @pl.when((a - d >= 0) & (a + 1 < rows))
        def _():
            kvhop(d).wait_send()

        if d > 0:
            @pl.when(a - d >= 0)
            def _():
                kvside(d).wait_send()


def specs(count):
    return [pl.BlockSpec(memory_space=pltpu.VMEM)] * count


def per_device(n, mixer_input, input_map, output_map, log_decay, query_rows, key_rows, value_rows):
    width = MIXER_HEADS * P_SIZE
    rows = n // 2
    sem = pltpu.SemaphoreType.DMA
    chunked = pltpu.VMEM((CHUNKS, N, CW), BF)
    big = GROUP * T
    return pl.pallas_call(
        functools.partial(kernel, n),
        out_shape=(
            jax.ShapeDtypeStruct((T, width), BF),
            jax.ShapeDtypeStruct((T, QH * DH), BF),
        ),
        in_specs=specs(7),
        out_specs=specs(2),
        scratch_shapes=[
            pltpu.VMEM((n, KV_ROWS, T), BF),
            pltpu.VMEM((2, CHUNKS, N, CW), F32),
            pltpu.VMEM((2, 1, HALF), F32),
            pltpu.VMEM((T, width), F32),
            pltpu.VMEM((T, T), F32),
            chunked, chunked, pltpu.VMEM((1, HALF), F32), chunked, chunked, chunked,
            pltpu.VMEM((2, CHUNKS, N, CW), BF),
            pltpu.VMEM((KVH, DH, big), BF),
            pltpu.VMEM((KVH, 1, big), F32),
            pltpu.VMEM((KVH, 1, big), F32),
            pltpu.VMEM((KVH, DH, big), F32),
            sem((CHUNKS,)), sem((CHUNKS,)), sem((2,)), sem((CHUNKS,)), sem((CHUNKS,)),
            sem((CHUNKS,)), sem((CHUNKS,)), sem((rows,)), sem((n,)), sem((rows,)),
        ],
        compiler_params=pltpu.CompilerParams(
            collective_id=0, has_side_effects=True, vmem_limit_bytes=VMEM_LIMIT
        ),
        name="mix_and_attend",
    )(mixer_input, input_map, output_map, log_decay.T, query_rows, key_rows.T, value_rows.T)


def solution(mesh):
    rows = P(("dp", "ctx"), None)
    return jax.shard_map(
        functools.partial(per_device, mesh.shape["ctx"]),
        mesh=mesh,
        in_specs=(rows,) * 7,
        out_specs=(rows, rows),
        check_vma=False,
    )
```

```python
import functools
import math

import jax
import jax.numpy as jnp
from jax import lax
from jax.experimental import pallas as pl
from jax.experimental.pallas import tpu as pltpu
from jax.sharding import PartitionSpec as P

MIXER_HEADS = 40
P_SIZE = 64
N = 128
QH = 32
KVH = 4
DH = 80
T = 128
GROUP = QH // KVH
KV_ROWS = 2 * KVH * DH
CHUNKS = 5
CW = 256
PAIRS = MIXER_HEADS // 2
HALF = MIXER_HEADS * P_SIZE // 2
EXP_SCALE = math.log2(math.e) / math.sqrt(DH)
MASKED = -1e30
MESH = pl.DeviceIdType.MESH
BF = jnp.bfloat16
F32 = jnp.float32
VMEM_LIMIT = 56 * 1024 * 1024


def iota(shape, dim):
    return lax.broadcasted_iota(jnp.int32, shape, dim)


def nt_dot(a, b):
    return lax.dot_general(a, b, (((1,), (1,)), ((), ())), preferred_element_type=F32)


def dot(a, b):
    return jnp.dot(a, b, preferred_element_type=F32)


def kernel(
    n, x_ref, in_ref, out_ref, ld_ref, q_ref, k_ref, v_ref, mix_ref, att_ref,
    kvall, u, f, inner, ecum_ref, usend, urecv, frecv, sin, sout, entsend, ent,
    qs, top, total, acc,
    us_sem, ur_sem, f_sem, ss_sem, sr_sem, es_sem, er_sem, kvs_sem, kvr_sem, px_sem,
):
    dp = lax.axis_index("dp")
    me = lax.axis_index("ctx")
    a, b = me // 2, me % 2
    rows = n // 2
    partner = (dp, a * 2 + 1 - b)
    ahead = (dp, lax.rem(a + 1, rows) * 2 + b)
    behind = (dp, lax.rem(a + rows - 1, rows) * 2 + b)
    first = b == 0

    def ucopy(c):
        return pltpu.make_async_remote_copy(
            src_ref=usend.at[c], dst_ref=urecv.at[c], send_sem=us_sem.at[c],
            recv_sem=ur_sem.at[c], device_id=partner, device_id_type=MESH)

    def fcopy():
        return pltpu.make_async_remote_copy(
            src_ref=f.at[1 - b], dst_ref=frecv, send_sem=f_sem.at[0],
            recv_sem=f_sem.at[1], device_id=partner, device_id_type=MESH)

    def scopy(c):
        return pltpu.make_async_remote_copy(
            src_ref=sout.at[c], dst_ref=sin.at[c], send_sem=ss_sem.at[c],
            recv_sem=sr_sem.at[c], device_id=ahead, device_id_type=MESH)

    def ecopy(c):
        return pltpu.make_async_remote_copy(
            src_ref=entsend.at[c], dst_ref=ent.at[b, c], send_sem=es_sem.at[c],
            recv_sem=er_sem.at[c], device_id=partner, device_id_type=MESH)

    def kvhop(d):
        block = me - 2 * d
        return pltpu.make_async_remote_copy(
            src_ref=kvall.at[block], dst_ref=kvall.at[block], send_sem=kvs_sem.at[d],
            recv_sem=kvr_sem.at[block], device_id=ahead, device_id_type=MESH)

    def kvside(d):
        block = me - 2 * d
        return pltpu.make_async_remote_copy(
            src_ref=kvall.at[block], dst_ref=kvall.at[block], send_sem=px_sem.at[d],
            recv_sem=kvr_sem.at[block], device_id=partner, device_id_type=MESH)

    def kvarrive(block):
        pltpu.make_async_copy(kvall.at[block], kvall.at[block], kvr_sem.at[block]).wait()

    barrier = pltpu.get_barrier_semaphore()
    for device in (partner, ahead, behind):
        pl.semaphore_signal(barrier, inc=1, device_id=device, device_id_type=MESH)
    kvall[me, : KVH * DH, :] = k_ref[...]
    kvall[me, KVH * DH :, :] = v_ref[...]
    pl.semaphore_wait(barrier, 3)

    @pl.when(a + 1 < rows)
    def _():
        kvhop(0).start()

    lower = iota((T, T), 0) >= iota((T, T), 1)
    triu = jnp.where(iota((T, T), 0) <= iota((T, T), 1), 1.0, 0.0).astype(F32)
    cum_t = jnp.dot(ld_ref[...], triu, precision=lax.Precision.HIGHEST, preferred_element_type=F32)
    cum = jnp.concatenate([cum_t, jnp.zeros((T - MIXER_HEADS, T), F32)], axis=0).T
    ecum = jnp.exp(cum)
    ecum_ref[...] = ecum
    match = jnp.where(lower, nt_dot(out_ref[...], in_ref[...]), 0.0)
    in_t = in_ref[...].astype(F32).T
    left = iota((T, T), 1) < P_SIZE
    last = ecum[T - 1 : T, :]
    for j in range(PAIRS):
        half, place = divmod(j, PAIRS // 2)
        f[half, :, place * T : (place + 1) * T] = jnp.where(
            left[:1], last[:, 2 * j : 2 * j + 1], last[:, 2 * j + 1 : 2 * j + 2]
        )
    fcopy().start()
    for c in range(CHUNKS):
        for half in range(2):
            for e in range(CW // T):
                j = (half * CHUNKS + c) * (CW // T) + e
                stack = []
                tails = []
                for h in (2 * j, 2 * j + 1):
                    row = cum_t[h : h + 1, :]
                    gap = jnp.minimum(cum[:, h : h + 1] - row, 0.0)
                    stack.append((match * jnp.exp(gap)).astype(BF))
                    tails.append((in_t * jnp.exp(row[:, T - 1 :] - row)).astype(BF))
                cols = slice(j * T, (j + 1) * T)
                out = dot(jnp.concatenate(stack + tails, axis=0), x_ref[:, cols])
                inner[:, cols] = jnp.where(left, out[:T], out[T : 2 * T])
                u[half, c, :, e * T : (e + 1) * T] = jnp.where(
                    left, out[2 * T : 3 * T], out[3 * T :]
                )
        usend[c] = u[1 - b, c].astype(BF)
        ucopy(c).start()
        if c == 0:
            @pl.when(first)
            def _():
                kvside(0).start()

    @pl.when(first)
    def _():
        kvall[me + 1] = jnp.zeros((KV_ROWS, T), BF)

    def hand_on(d):
        @pl.when(a - d >= 0)
        def _():
            kvarrive(me - 2 * d)
            kvside(d).start()

            @pl.when(a + 1 < rows)
            def _():
                kvhop(d).start()

    def chain():
        fcopy().wait_recv()
        f_own = f[b]
        f_other = frecv[...]
        f_early = jnp.where(first, f_own, f_other)
        f_late = jnp.where(first, f_other, f_own)
        f_pair = f_early * f_late
        for c in range(CHUNKS):
            lanes = slice(c * CW, (c + 1) * CW)
            ucopy(c).wait_recv()
            u_own = u[b, c]
            u_other = urecv[c].astype(F32)
            early = jnp.where(first, u_own, u_other)
            late = jnp.where(first, u_other, u_own)
            pair = f_late[:, lanes] * early + late

            @pl.when(a == 0)
            def _():
                sin[c] = jnp.zeros((T, CW), BF)

            @pl.when(a > 0)
            def _():
                scopy(c).wait_recv()

            state = sin[c].astype(F32)

            @pl.when(a + 1 < rows)
            def _():
                sout[c] = (f_pair[:, lanes] * state + pair).astype(BF)
                scopy(c).start()

            middle = f_early[:, lanes] * state + early
            entsend[c] = jnp.where(first, middle, state).astype(BF)
            ecopy(c).start()
            ent[b, c] = jnp.where(first, state, middle).astype(BF)

    wide = 2 * T

    def attend(p, opening):
        def group(g, _):
            kc = pl.ds(pl.multiple_of(g * DH, 16), DH)
            vc = pl.ds(pl.multiple_of((KVH + g) * DH, 16), DH)
            keys = jnp.concatenate([kvall[2 * p, kc, :], kvall[2 * p + 1, kc, :]], axis=1)
            values = jnp.concatenate([kvall[2 * p, vc, :], kvall[2 * p + 1, vc, :]], axis=1)
            if opening:
                width = GROUP * DH
                q = q_ref[:, pl.ds(pl.multiple_of(g * width, T), width)]
                queries = jnp.concatenate([q[:, r * DH : (r + 1) * DH] for r in range(GROUP)], axis=0)
                qs[g] = queries
                shown = iota((T, wide), 1) <= iota((T, wide), 0) + b * T
            else:
                queries = qs[g]
                old_top = top[g]
                old_total = total[g]
                old_acc = acc[g]
            scores = dot(queries, keys)
            peaks, totals, shrinks, expos = [], [], [], []
            for r in range(GROUP):
                at = slice(r * T, (r + 1) * T)
                s = scores[at]
                if opening:
                    s = jnp.where(shown, s, MASKED)
                peak = jnp.max(jnp.maximum(s[:, :T], s[:, T:]), axis=1, keepdims=True)
                if opening:
                    peak = jnp.broadcast_to(peak, (T, T))
                else:
                    peak = jnp.maximum(old_top[at], peak)
                    shrinks.append(jnp.exp2((old_top[at] - peak) * EXP_SCALE))
                peaks.append(peak)
                e0 = jnp.exp2((s[:, :T] - peak) * EXP_SCALE)
                e1 = jnp.exp2((s[:, T:] - peak) * EXP_SCALE)
                totals.append(e0 + e1)
                expos.append(jnp.concatenate([e0.astype(BF), e1.astype(BF)], axis=1))
            summed = nt_dot(jnp.concatenate(expos, axis=0), values)
            for r in range(GROUP):
                at = slice(r * T, (r + 1) * T)
                top[g, at, :] = peaks[r]
                if opening:
                    total[g, at, :] = totals[r]
                    acc[g, at, :] = summed[at]
                else:
                    total[g, at, :] = old_total[at] * shrinks[r] + totals[r]
                    acc[g, at, :] = old_acc[at] * shrinks[r][:, :DH] + summed[at]
            return 0

        lax.fori_loop(0, KVH, group, 0)

    def finish(g, _):
        width = GROUP * DH
        outs = []
        for r in range(GROUP):
            at = slice(r * T, (r + 1) * T)
            outs.append((acc[g, at, :] / jnp.sum(total[g, at, :], axis=1, keepdims=True)).astype(BF))
        att_ref[:, pl.ds(pl.multiple_of(g * width, T), width)] = jnp.concatenate(outs, axis=1)
        return 0

    hand_on(1)

    @pl.when(a <= 1)
    def _():
        chain()

    @pl.when(b == 1)
    def _():
        kvarrive(me - 1)

    attend(a, True)

    def step(d, _):
        hand_on(d + 1)

        @pl.when((a >= 2) & (d == jnp.where(a == 2, 1, jnp.minimum(a, 3))))
        def _():
            chain()

        kvarrive((a - d) * 2 + 1 - b)
        attend(a - d, False)
        return 0

    lax.fori_loop(1, a + 1, step, 0)
    lax.fori_loop(0, KVH, finish, 0)

    for c in range(CHUNKS):
        ecopy(c).wait_recv()
        for half in range(2):
            carried = dot(out_ref[...], ent[half, c])
            for e in range(CW // T):
                j = (half * CHUNKS + c) * (CW // T) + e
                factor = jnp.where(
                    left, ecum_ref[:, 2 * j : 2 * j + 1], ecum_ref[:, 2 * j + 1 : 2 * j + 2]
                )
                cols = slice(j * T, (j + 1) * T)
                mix_ref[:, cols] = (
                    inner[:, cols] + carried[:, e * T : (e + 1) * T] * factor
                ).astype(BF)

    fcopy().wait_send()
    for c in range(CHUNKS):
        ucopy(c).wait_send()
        ecopy(c).wait_send()

        @pl.when(a + 1 < rows)
        def _():
            scopy(c).wait_send()

    @pl.when(first)
    def _():
        kvside(0).wait_send()

    for d in range(rows):
        @pl.when((a - d >= 0) & (a + 1 < rows))
        def _():
            kvhop(d).wait_send()

        if d > 0:
            @pl.when(a - d >= 0)
            def _():
                kvside(d).wait_send()


def deliver_kernel(mix_ref, att_ref, mix_out, att_out, done):
    copies = []
    for k, (src, dst) in enumerate(((mix_ref, mix_out), (att_ref, att_out))):
        for half in range(2):
            at = pl.ds(half * (T // 2), T // 2)
            copies.append(pltpu.make_async_copy(src.at[at], dst.at[at], done.at[2 * k + half]))
    for copy in copies:
        copy.start()
    for copy in copies:
        copy.wait()


def specs(count):
    return [pl.BlockSpec(memory_space=pltpu.VMEM)] * count


def per_device(n, mixer_input, input_map, output_map, log_decay, query_rows, key_rows, value_rows):
    width = MIXER_HEADS * P_SIZE
    rows = n // 2
    sem = pltpu.SemaphoreType.DMA
    chunked = pltpu.VMEM((CHUNKS, N, CW), BF)
    big = GROUP * T
    mixed, attended = pl.pallas_call(
        functools.partial(kernel, n),
        out_shape=(
            jax.ShapeDtypeStruct((T, width), BF),
            jax.ShapeDtypeStruct((T, QH * DH), BF),
        ),
        in_specs=specs(7),
        out_specs=specs(2),
        scratch_shapes=[
            pltpu.VMEM((n, KV_ROWS, T), BF),
            pltpu.VMEM((2, CHUNKS, N, CW), F32),
            pltpu.VMEM((2, 1, HALF), F32),
            pltpu.VMEM((T, width), F32),
            pltpu.VMEM((T, T), F32),
            chunked, chunked, pltpu.VMEM((1, HALF), F32), chunked, chunked, chunked,
            pltpu.VMEM((2, CHUNKS, N, CW), BF),
            pltpu.VMEM((KVH, big, DH), BF),
            pltpu.VMEM((KVH, big, T), F32),
            pltpu.VMEM((KVH, big, T), F32),
            pltpu.VMEM((KVH, big, DH), F32),
            sem((CHUNKS,)), sem((CHUNKS,)), sem((2,)), sem((CHUNKS,)), sem((CHUNKS,)),
            sem((CHUNKS,)), sem((CHUNKS,)), sem((rows,)), sem((n,)), sem((rows,)),
        ],
        compiler_params=pltpu.CompilerParams(
            collective_id=0, has_side_effects=True, vmem_limit_bytes=VMEM_LIMIT
        ),
        name="mix_and_attend",
    )(mixer_input, input_map, output_map, log_decay.T, query_rows, key_rows.T, value_rows.T)
    return pl.pallas_call(
        deliver_kernel,
        out_shape=(
            jax.ShapeDtypeStruct((T, width), BF),
            jax.ShapeDtypeStruct((T, QH * DH), BF),
        ),
        in_specs=[pl.BlockSpec(memory_space=pl.ANY)] * 2,
        out_specs=[pl.BlockSpec(memory_space=pl.ANY)] * 2,
        scratch_shapes=[sem((4,))],
        name="deliver",
    )(mixed, attended)


def solution(mesh):
    rows = P(("dp", "ctx"), None)
    return jax.shard_map(
        functools.partial(per_device, mesh.shape["ctx"]),
        mesh=mesh,
        in_specs=(rows,) * 7,
        out_specs=(rows, rows),
        check_vma=False,
    )
```

```python
import functools
import math

import jax
import jax.numpy as jnp
from jax import lax
from jax.experimental import pallas as pl
from jax.experimental.pallas import tpu as pltpu
from jax.sharding import PartitionSpec as P

MIXER_HEADS = 40
P_SIZE = 64
N = 128
QH = 32
KVH = 4
DH = 80
T = 128
GROUP = QH // KVH
KV_ROWS = 2 * KVH * DH
CHUNKS = 5
NEAR = 3
CW = 256
PAIRS = MIXER_HEADS // 2
HALF = MIXER_HEADS * P_SIZE // 2
EXP_SCALE = math.log2(math.e) / math.sqrt(DH)
MASKED = -1e30
MESH = pl.DeviceIdType.MESH
BF = jnp.bfloat16
F32 = jnp.float32
VMEM_LIMIT = 56 * 1024 * 1024


def iota(shape, dim):
    return lax.broadcasted_iota(jnp.int32, shape, dim)


def nt_dot(a, b):
    return lax.dot_general(a, b, (((1,), (1,)), ((), ())), preferred_element_type=F32)


def dot(a, b):
    return jnp.dot(a, b, preferred_element_type=F32)


def kernel(
    n, x_ref, in_ref, out_ref, ld_ref, q_ref, k_ref, v_ref, mix_ref, att_ref,
    kvall, u, f, inner, ecum_ref, usend, urecv, frecv, sin, sout, entsend, ent,
    qs, top, total, acc,
    us_sem, ur_sem, f_sem, ss_sem, sr_sem, es_sem, er_sem, kvs_sem, kvr_sem, px_sem, far_sem,
):
    dp = lax.axis_index("dp")
    me = lax.axis_index("ctx")
    a, b = me // 2, me % 2
    rows = n // 2
    partner = (dp, a * 2 + 1 - b)
    ahead = (dp, lax.rem(a + 1, rows) * 2 + b)
    behind = (dp, lax.rem(a + rows - 1, rows) * 2 + b)
    first = b == 0

    def ucopy(c):
        return pltpu.make_async_remote_copy(
            src_ref=usend.at[c], dst_ref=urecv.at[c], send_sem=us_sem.at[c],
            recv_sem=ur_sem.at[c], device_id=partner, device_id_type=MESH)

    def fcopy():
        return pltpu.make_async_remote_copy(
            src_ref=f.at[1 - b], dst_ref=frecv, send_sem=f_sem.at[0],
            recv_sem=f_sem.at[1], device_id=partner, device_id_type=MESH)

    def scopy(c):
        return pltpu.make_async_remote_copy(
            src_ref=sout.at[c], dst_ref=sin.at[c], send_sem=ss_sem.at[c],
            recv_sem=sr_sem.at[c], device_id=ahead, device_id_type=MESH)

    def ecopy(c):
        return pltpu.make_async_remote_copy(
            src_ref=entsend.at[c], dst_ref=ent.at[b, c], send_sem=es_sem.at[c],
            recv_sem=er_sem.at[c], device_id=partner, device_id_type=MESH)

    def kvhop(d):
        block = me - 2 * d
        return pltpu.make_async_remote_copy(
            src_ref=kvall.at[block], dst_ref=kvall.at[block], send_sem=kvs_sem.at[d],
            recv_sem=kvr_sem.at[block], device_id=ahead, device_id_type=MESH)

    def kvside(d):
        block = me - 2 * d
        return pltpu.make_async_remote_copy(
            src_ref=kvall.at[block], dst_ref=kvall.at[block], send_sem=px_sem.at[d],
            recv_sem=kvr_sem.at[block], device_id=partner, device_id_type=MESH)

    def kvfar(d):
        return pltpu.make_async_remote_copy(
            src_ref=kvall.at[me], dst_ref=kvall.at[me], send_sem=far_sem.at[d],
            recv_sem=kvr_sem.at[me], device_id=(dp, lax.rem(a + d, rows) * 2 + 1 - b),
            device_id_type=MESH)

    def kvarrive(block):
        pltpu.make_async_copy(kvall.at[block], kvall.at[block], kvr_sem.at[block]).wait()

    barrier = pltpu.get_barrier_semaphore()
    across = [(dp, lax.rem(a + d, rows) * 2 + 1 - b) for d in range(1, rows)] if rows > NEAR else []
    for device in [partner, ahead, behind] + across:
        pl.semaphore_signal(barrier, inc=1, device_id=device, device_id_type=MESH)
    kvall[me, : KVH * DH, :] = k_ref[...]
    kvall[me, KVH * DH :, :] = v_ref[...]
    pl.semaphore_wait(barrier, 3 + len(across))

    @pl.when(a + 1 < rows)
    def _():
        kvhop(0).start()

    for d in range(NEAR, rows):
        @pl.when(a + d < rows)
        def _():
            kvfar(d).start()

    @pl.when(first & (a >= 2))
    def _():
        kvside(0).start()

    lower = iota((T, T), 0) >= iota((T, T), 1)
    triu = jnp.where(iota((T, T), 0) <= iota((T, T), 1), 1.0, 0.0).astype(F32)
    cum_t = jnp.dot(ld_ref[...], triu, precision=lax.Precision.HIGHEST, preferred_element_type=F32)
    cum = jnp.concatenate([cum_t, jnp.zeros((T - MIXER_HEADS, T), F32)], axis=0).T
    ecum = jnp.exp(cum)
    ecum_ref[...] = ecum
    match = jnp.where(lower, nt_dot(out_ref[...], in_ref[...]), 0.0)
    in_t = in_ref[...].astype(F32).T
    left = iota((T, T), 1) < P_SIZE
    last = ecum[T - 1 : T, :]
    for j in range(PAIRS):
        half, place = divmod(j, PAIRS // 2)
        f[half, :, place * T : (place + 1) * T] = jnp.where(
            left[:1], last[:, 2 * j : 2 * j + 1], last[:, 2 * j + 1 : 2 * j + 2]
        )
    fcopy().start()
    for c in range(CHUNKS):
        for half in range(2):
            for e in range(CW // T):
                j = (half * CHUNKS + c) * (CW // T) + e
                stack = []
                tails = []
                for h in (2 * j, 2 * j + 1):
                    row = cum_t[h : h + 1, :]
                    gap = jnp.minimum(cum[:, h : h + 1] - row, 0.0)
                    stack.append((match * jnp.exp(gap)).astype(BF))
                    tails.append((in_t * jnp.exp(row[:, T - 1 :] - row)).astype(BF))
                cols = slice(j * T, (j + 1) * T)
                out = dot(jnp.concatenate(stack + tails, axis=0), x_ref[:, cols])
                inner[:, cols] = jnp.where(left, out[:T], out[T : 2 * T])
                u[half, c, :, e * T : (e + 1) * T] = jnp.where(
                    left, out[2 * T : 3 * T], out[3 * T :]
                )
        usend[c] = u[1 - b, c].astype(BF)
        ucopy(c).start()
        if c == 0:
            @pl.when(first & (a < 2))
            def _():
                kvside(0).start()

    @pl.when(first)
    def _():
        kvall[me + 1] = jnp.zeros((KV_ROWS, T), BF)

    def hand_on(d):
        @pl.when(a - d >= 0)
        def _():
            kvarrive(me - 2 * d)

            @pl.when(d < NEAR)
            def _():
                kvside(d).start()

            @pl.when(a + 1 < rows)
            def _():
                kvhop(d).start()

    def chain():
        fcopy().wait_recv()
        f_own = f[b]
        f_other = frecv[...]
        f_early = jnp.where(first, f_own, f_other)
        f_late = jnp.where(first, f_other, f_own)
        f_pair = f_early * f_late
        for c in range(CHUNKS):
            lanes = slice(c * CW, (c + 1) * CW)
            ucopy(c).wait_recv()
            u_own = u[b, c]
            u_other = urecv[c].astype(F32)
            early = jnp.where(first, u_own, u_other)
            late = jnp.where(first, u_other, u_own)
            pair = f_late[:, lanes] * early + late

            @pl.when(a == 0)
            def _():
                sin[c] = jnp.zeros((T, CW), BF)

            @pl.when(a > 0)
            def _():
                scopy(c).wait_recv()

            state = sin[c].astype(F32)

            @pl.when(a + 1 < rows)
            def _():
                sout[c] = (f_pair[:, lanes] * state + pair).astype(BF)
                scopy(c).start()

            middle = f_early[:, lanes] * state + early
            entsend[c] = jnp.where(first, middle, state).astype(BF)
            ecopy(c).start()
            ent[b, c] = jnp.where(first, state, middle).astype(BF)

    wide = 2 * T

    def attend(p, opening):
        def group(g, _):
            kc = pl.ds(pl.multiple_of(g * DH, 16), DH)
            vc = pl.ds(pl.multiple_of((KVH + g) * DH, 16), DH)
            keys = jnp.concatenate([kvall[2 * p, kc, :], kvall[2 * p + 1, kc, :]], axis=1)
            values = jnp.concatenate([kvall[2 * p, vc, :], kvall[2 * p + 1, vc, :]], axis=1)
            if opening:
                width = GROUP * DH
                q = q_ref[:, pl.ds(pl.multiple_of(g * width, T), width)]
                queries = jnp.concatenate([q[:, r * DH : (r + 1) * DH] for r in range(GROUP)], axis=0)
                qs[g] = queries
                shown = iota((T, wide), 1) <= iota((T, wide), 0) + b * T
            else:
                queries = qs[g]
                old_top = top[g]
                old_total = total[g]
                old_acc = acc[g]
            scores = dot(queries, keys)
            peaks, totals, shrinks, expos = [], [], [], []
            for r in range(GROUP):
                at = slice(r * T, (r + 1) * T)
                s = scores[at]
                if opening:
                    s = jnp.where(shown, s, MASKED)
                peak = jnp.max(jnp.maximum(s[:, :T], s[:, T:]), axis=1, keepdims=True)
                if opening:
                    peak = jnp.broadcast_to(peak, (T, T))
                else:
                    peak = jnp.maximum(old_top[at], peak)
                    shrinks.append(jnp.exp2((old_top[at] - peak) * EXP_SCALE))
                peaks.append(peak)
                e0 = jnp.exp2((s[:, :T] - peak) * EXP_SCALE)
                e1 = jnp.exp2((s[:, T:] - peak) * EXP_SCALE)
                totals.append(e0 + e1)
                expos.append(jnp.concatenate([e0.astype(BF), e1.astype(BF)], axis=1))
            summed = nt_dot(jnp.concatenate(expos, axis=0), values)
            for r in range(GROUP):
                at = slice(r * T, (r + 1) * T)
                top[g, at, :] = peaks[r]
                if opening:
                    total[g, at, :] = totals[r]
                    acc[g, at, :] = summed[at]
                else:
                    total[g, at, :] = old_total[at] * shrinks[r] + totals[r]
                    acc[g, at, :] = old_acc[at] * shrinks[r][:, :DH] + summed[at]
            return 0

        lax.fori_loop(0, KVH, group, 0)

    def finish(g, _):
        width = GROUP * DH
        outs = []
        for r in range(GROUP):
            at = slice(r * T, (r + 1) * T)
            outs.append((acc[g, at, :] / jnp.sum(total[g, at, :], axis=1, keepdims=True)).astype(BF))
        att_ref[:, pl.ds(pl.multiple_of(g * width, T), width)] = jnp.concatenate(outs, axis=1)
        return 0

    hand_on(1)

    @pl.when(a <= 1)
    def _():
        chain()

    @pl.when(b == 1)
    def _():
        kvarrive(me - 1)

    attend(a, True)

    def step(d, _):
        hand_on(d + 1)

        @pl.when((a >= 2) & (d == jnp.where(a == 2, 1, jnp.minimum(a, 3))))
        def _():
            chain()

        kvarrive((a - d) * 2 + 1 - b)
        attend(a - d, False)
        return 0

    lax.fori_loop(1, a + 1, step, 0)
    lax.fori_loop(0, KVH, finish, 0)

    for c in range(CHUNKS):
        ecopy(c).wait_recv()
        for half in range(2):
            carried = dot(out_ref[...], ent[half, c])
            for e in range(CW // T):
                j = (half * CHUNKS + c) * (CW // T) + e
                factor = jnp.where(
                    left, ecum_ref[:, 2 * j : 2 * j + 1], ecum_ref[:, 2 * j + 1 : 2 * j + 2]
                )
                cols = slice(j * T, (j + 1) * T)
                mix_ref[:, cols] = (
                    inner[:, cols] + carried[:, e * T : (e + 1) * T] * factor
                ).astype(BF)

    fcopy().wait_send()
    for c in range(CHUNKS):
        ucopy(c).wait_send()
        ecopy(c).wait_send()

        @pl.when(a + 1 < rows)
        def _():
            scopy(c).wait_send()

    @pl.when(first)
    def _():
        kvside(0).wait_send()

    for d in range(rows):
        @pl.when((a - d >= 0) & (a + 1 < rows))
        def _():
            kvhop(d).wait_send()

        if 0 < d < NEAR:
            @pl.when(a - d >= 0)
            def _():
                kvside(d).wait_send()

        if d >= NEAR:
            @pl.when(a + d < rows)
            def _():
                kvfar(d).wait_send()


def deliver_kernel(mix_ref, att_ref, mix_out, att_out):
    mix_out[...] = mix_ref[...]
    att_out[...] = att_ref[...]


def specs(count):
    return [pl.BlockSpec(memory_space=pltpu.VMEM)] * count


def per_device(n, mixer_input, input_map, output_map, log_decay, query_rows, key_rows, value_rows):
    width = MIXER_HEADS * P_SIZE
    rows = n // 2
    sem = pltpu.SemaphoreType.DMA
    chunked = pltpu.VMEM((CHUNKS, N, CW), BF)
    big = GROUP * T
    mixed, attended = pl.pallas_call(
        functools.partial(kernel, n),
        out_shape=(
            jax.ShapeDtypeStruct((T, width), BF),
            jax.ShapeDtypeStruct((T, QH * DH), BF),
        ),
        in_specs=specs(7),
        out_specs=specs(2),
        scratch_shapes=[
            pltpu.VMEM((n, KV_ROWS, T), BF),
            pltpu.VMEM((2, CHUNKS, N, CW), F32),
            pltpu.VMEM((2, 1, HALF), F32),
            pltpu.VMEM((T, width), F32),
            pltpu.VMEM((T, T), F32),
            chunked, chunked, pltpu.VMEM((1, HALF), F32), chunked, chunked, chunked,
            pltpu.VMEM((2, CHUNKS, N, CW), BF),
            pltpu.VMEM((KVH, big, DH), BF),
            pltpu.VMEM((KVH, big, T), F32),
            pltpu.VMEM((KVH, big, T), F32),
            pltpu.VMEM((KVH, big, DH), F32),
            sem((CHUNKS,)), sem((CHUNKS,)), sem((2,)), sem((CHUNKS,)), sem((CHUNKS,)),
            sem((CHUNKS,)), sem((CHUNKS,)), sem((rows,)), sem((n,)), sem((NEAR,)), sem((rows,)),
        ],
        compiler_params=pltpu.CompilerParams(
            collective_id=0, has_side_effects=True, vmem_limit_bytes=VMEM_LIMIT
        ),
        name="mix_and_attend",
    )(mixer_input, input_map, output_map, log_decay.T, query_rows, key_rows.T, value_rows.T)
    return pl.pallas_call(
        deliver_kernel,
        out_shape=(
            jax.ShapeDtypeStruct((T, width), BF),
            jax.ShapeDtypeStruct((T, QH * DH), BF),
        ),
        in_specs=specs(2),
        out_specs=specs(2),
        name="deliver",
    )(mixed, attended)


def solution(mesh):
    rows = P(("dp", "ctx"), None)
    return jax.shard_map(
        functools.partial(per_device, mesh.shape["ctx"]),
        mesh=mesh,
        in_specs=(rows,) * 7,
        out_specs=(rows, rows),
        check_vma=False,
    )
```

```python
import functools
import math

import jax
import jax.numpy as jnp
from jax import lax
from jax.experimental import pallas as pl
from jax.experimental.pallas import tpu as pltpu
from jax.sharding import PartitionSpec as P

MIXER_HEADS = 40
P_SIZE = 64
N = 128
QH = 32
KVH = 4
DH = 80
WITH_SUM = 96
T = 128
GROUP = QH // KVH
KV_ROWS = 2 * KVH * DH
CHUNKS = 5
CW = 256
PAIRS = MIXER_HEADS // 2
HALF = MIXER_HEADS * P_SIZE // 2
EXP_SCALE = math.log2(math.e) / math.sqrt(DH)
MASKED = -1e30
MESH = pl.DeviceIdType.MESH
BF = jnp.bfloat16
F32 = jnp.float32
VMEM_LIMIT = 56 * 1024 * 1024


def iota(shape, dim):
    return lax.broadcasted_iota(jnp.int32, shape, dim)


def nt_dot(a, b):
    return lax.dot_general(a, b, (((1,), (1,)), ((), ())), preferred_element_type=F32)


def dot(a, b):
    return jnp.dot(a, b, preferred_element_type=F32)


def kernel(
    n, x_ref, in_ref, out_ref, ld_ref, q_ref, k_ref, v_ref, mix_ref, att_ref,
    kvall, u, f, inner, ecum_ref, usend, urecv, frecv, sin, sout, entsend, ent,
    qs, top, acc,
    us_sem, ur_sem, f_sem, ss_sem, sr_sem, es_sem, er_sem, kvs_sem, kvr_sem, px_sem,
):
    dp = lax.axis_index("dp")
    me = lax.axis_index("ctx")
    a, b = me // 2, me % 2
    rows = n // 2
    partner = (dp, a * 2 + 1 - b)
    ahead = (dp, lax.rem(a + 1, rows) * 2 + b)
    behind = (dp, lax.rem(a + rows - 1, rows) * 2 + b)
    first = b == 0

    def ucopy(c):
        return pltpu.make_async_remote_copy(
            src_ref=usend.at[c], dst_ref=urecv.at[c], send_sem=us_sem.at[c],
            recv_sem=ur_sem.at[c], device_id=partner, device_id_type=MESH)

    def fcopy():
        return pltpu.make_async_remote_copy(
            src_ref=f.at[1 - b], dst_ref=frecv, send_sem=f_sem.at[0],
            recv_sem=f_sem.at[1], device_id=partner, device_id_type=MESH)

    def scopy(c):
        return pltpu.make_async_remote_copy(
            src_ref=sout.at[c], dst_ref=sin.at[c], send_sem=ss_sem.at[c],
            recv_sem=sr_sem.at[c], device_id=ahead, device_id_type=MESH)

    def ecopy(c):
        return pltpu.make_async_remote_copy(
            src_ref=entsend.at[c], dst_ref=ent.at[b, c], send_sem=es_sem.at[c],
            recv_sem=er_sem.at[c], device_id=partner, device_id_type=MESH)

    def kvhop(d):
        block = me - 2 * d
        return pltpu.make_async_remote_copy(
            src_ref=kvall.at[block], dst_ref=kvall.at[block], send_sem=kvs_sem.at[d],
            recv_sem=kvr_sem.at[block], device_id=ahead, device_id_type=MESH)

    def kvside(d):
        block = me - 2 * d
        return pltpu.make_async_remote_copy(
            src_ref=kvall.at[block], dst_ref=kvall.at[block], send_sem=px_sem.at[d],
            recv_sem=kvr_sem.at[block], device_id=partner, device_id_type=MESH)

    def kvarrive(block):
        pltpu.make_async_copy(kvall.at[block], kvall.at[block], kvr_sem.at[block]).wait()

    barrier = pltpu.get_barrier_semaphore()
    for device in (partner, ahead, behind):
        pl.semaphore_signal(barrier, inc=1, device_id=device, device_id_type=MESH)
    kvall[me, : KVH * DH, :] = k_ref[...]
    kvall[me, KVH * DH :, :] = v_ref[...]
    pl.semaphore_wait(barrier, 3)

    @pl.when(a + 1 < rows)
    def _():
        kvhop(0).start()

    lower = iota((T, T), 0) >= iota((T, T), 1)
    triu = jnp.where(iota((T, T), 0) <= iota((T, T), 1), 1.0, 0.0).astype(F32)
    cum_t = jnp.dot(ld_ref[...], triu, precision=lax.Precision.HIGHEST, preferred_element_type=F32)
    cum = jnp.concatenate([cum_t, jnp.zeros((T - MIXER_HEADS, T), F32)], axis=0).T
    ecum = jnp.exp(cum)
    ecum_ref[...] = ecum
    match = jnp.where(lower, nt_dot(out_ref[...], in_ref[...]), 0.0)
    in_t = in_ref[...].astype(F32).T
    left = iota((T, T), 1) < P_SIZE
    last = ecum[T - 1 : T, :]
    for j in range(PAIRS):
        half, place = divmod(j, PAIRS // 2)
        f[half, :, place * T : (place + 1) * T] = jnp.where(
            left[:1], last[:, 2 * j : 2 * j + 1], last[:, 2 * j + 1 : 2 * j + 2]
        )
    fcopy().start()
    for c in range(CHUNKS):
        for half in range(2):
            for e in range(CW // T):
                j = (half * CHUNKS + c) * (CW // T) + e
                stack = []
                tails = []
                for h in (2 * j, 2 * j + 1):
                    row = cum_t[h : h + 1, :]
                    gap = jnp.minimum(cum[:, h : h + 1] - row, 0.0)
                    stack.append((match * jnp.exp(gap)).astype(BF))
                    tails.append((in_t * jnp.exp(row[:, T - 1 :] - row)).astype(BF))
                cols = slice(j * T, (j + 1) * T)
                out = dot(jnp.concatenate(stack + tails, axis=0), x_ref[:, cols])
                inner[:, cols] = jnp.where(left, out[:T], out[T : 2 * T])
                u[half, c, :, e * T : (e + 1) * T] = jnp.where(
                    left, out[2 * T : 3 * T], out[3 * T :]
                )
        usend[c] = u[1 - b, c].astype(BF)
        ucopy(c).start()
        if c == 0:
            @pl.when(first)
            def _():
                kvside(0).start()

    @pl.when(first)
    def _():
        kvall[me + 1] = jnp.zeros((KV_ROWS, T), BF)

    def hand_on(d):
        @pl.when(a - d >= 0)
        def _():
            kvarrive(me - 2 * d)
            kvside(d).start()

            @pl.when(a + 1 < rows)
            def _():
                kvhop(d).start()

    def chain():
        fcopy().wait_recv()
        f_own = f[b]
        f_other = frecv[...]
        f_early = jnp.where(first, f_own, f_other)
        f_late = jnp.where(first, f_other, f_own)
        f_pair = f_early * f_late
        for c in range(CHUNKS):
            lanes = slice(c * CW, (c + 1) * CW)
            ucopy(c).wait_recv()
            u_own = u[b, c]
            u_other = urecv[c].astype(F32)
            early = jnp.where(first, u_own, u_other)
            late = jnp.where(first, u_other, u_own)
            pair = f_late[:, lanes] * early + late

            @pl.when(a == 0)
            def _():
                sin[c] = jnp.zeros((T, CW), BF)

            @pl.when(a > 0)
            def _():
                scopy(c).wait_recv()

            state = sin[c].astype(F32)

            @pl.when(a + 1 < rows)
            def _():
                sout[c] = (f_pair[:, lanes] * state + pair).astype(BF)
                scopy(c).start()

            middle = f_early[:, lanes] * state + early
            entsend[c] = jnp.where(first, middle, state).astype(BF)
            ecopy(c).start()
            ent[b, c] = jnp.where(first, state, middle).astype(BF)

    chunk = 2 * T
    parts = GROUP * T // chunk

    def attend(p, opening):
        def group(g, _):
            kc = pl.ds(pl.multiple_of(g * DH, 16), DH)
            vc = pl.ds(pl.multiple_of((KVH + g) * DH, 16), DH)
            keys = jnp.concatenate([kvall[2 * p, kc, :], kvall[2 * p + 1, kc, :]], axis=1)
            values = jnp.concatenate([kvall[2 * p, vc, :], kvall[2 * p + 1, vc, :]], axis=1)
            values = jnp.concatenate([values, jnp.ones((WITH_SUM - DH, 2 * T), BF)], axis=0)
            if opening:
                width = GROUP * DH
                q = q_ref[:, pl.ds(pl.multiple_of(g * width, T), width)]
                for r in range(GROUP):
                    qs[g, r * T : (r + 1) * T, :] = q[:, r * DH : (r + 1) * DH]
            for r in range(parts):
                at = slice(r * chunk, (r + 1) * chunk)
                s = dot(qs[g, at, :], keys)
                if opening:
                    shown = iota((chunk, chunk), 1) <= (iota((chunk, chunk), 0) % T) + b * T
                    s = jnp.where(shown, s, MASKED)
                peak = jnp.max(jnp.maximum(s[:, :T], s[:, T:]), axis=1, keepdims=True)
                if not opening:
                    old = top[g, at, :]
                    peak = jnp.maximum(old, peak)
                    shrink = jnp.exp2((old - peak) * EXP_SCALE)
                else:
                    peak = jnp.broadcast_to(peak, (chunk, T))
                top[g, at, :] = peak
                e0 = jnp.exp2((s[:, :T] - peak) * EXP_SCALE)
                e1 = jnp.exp2((s[:, T:] - peak) * EXP_SCALE)
                e = jnp.concatenate([e0.astype(BF), e1.astype(BF)], axis=1)
                summed = nt_dot(e, values)
                if opening:
                    acc[g, at, :] = summed
                else:
                    acc[g, at, :] = acc[g, at, :] * shrink[:, :WITH_SUM] + summed
            return 0

        lax.fori_loop(0, KVH, group, 0)

    def finish(g, _):
        width = GROUP * DH
        outs = []
        for r in range(GROUP):
            at = slice(r * T, (r + 1) * T)
            whole = acc[g, at, :]
            outs.append((whole[:, :DH] / whole[:, DH : DH + 1]).astype(BF))
        att_ref[:, pl.ds(pl.multiple_of(g * width, T), width)] = jnp.concatenate(outs, axis=1)
        return 0

    chain_at = min(2, rows - 1)
    for d in range(rows):
        if d + 1 < rows:
            hand_on(d + 1)
        when = {0: a <= 1, chain_at: a > chain_at}.get(d, a == d + 1)
        if d <= chain_at:
            pl.when(when)(chain)

        @pl.when((b == 1) if d == 0 else (a - d >= 0))
        def _():
            kvarrive((a - d) * 2 + 1 - b)

        if d == 0:
            attend(a, True)
        else:
            @pl.when(a - d >= 0)
            def _():
                attend(a - d, False)

    lax.fori_loop(0, KVH, finish, 0)

    for c in range(CHUNKS):
        ecopy(c).wait_recv()
        for half in range(2):
            carried = dot(out_ref[...], ent[half, c])
            for e in range(CW // T):
                j = (half * CHUNKS + c) * (CW // T) + e
                factor = jnp.where(
                    left, ecum_ref[:, 2 * j : 2 * j + 1], ecum_ref[:, 2 * j + 1 : 2 * j + 2]
                )
                cols = slice(j * T, (j + 1) * T)
                mix_ref[:, cols] = (
                    inner[:, cols] + carried[:, e * T : (e + 1) * T] * factor
                ).astype(BF)

    fcopy().wait_send()
    for c in range(CHUNKS):
        ucopy(c).wait_send()
        ecopy(c).wait_send()

        @pl.when(a + 1 < rows)
        def _():
            scopy(c).wait_send()

    @pl.when(first)
    def _():
        kvside(0).wait_send()

    for d in range(rows):
        @pl.when((a - d >= 0) & (a + 1 < rows))
        def _():
            kvhop(d).wait_send()

        if d > 0:
            @pl.when(a - d >= 0)
            def _():
                kvside(d).wait_send()


def deliver_kernel(mix_ref, att_ref, mix_out, att_out):
    mix_out[...] = mix_ref[...]
    att_out[...] = att_ref[...]


def specs(count):
    return [pl.BlockSpec(memory_space=pltpu.VMEM)] * count


def per_device(n, mixer_input, input_map, output_map, log_decay, query_rows, key_rows, value_rows):
    width = MIXER_HEADS * P_SIZE
    rows = n // 2
    sem = pltpu.SemaphoreType.DMA
    chunked = pltpu.VMEM((CHUNKS, N, CW), BF)
    big = GROUP * T
    mixed, attended = pl.pallas_call(
        functools.partial(kernel, n),
        out_shape=(
            jax.ShapeDtypeStruct((T, width), BF),
            jax.ShapeDtypeStruct((T, QH * DH), BF),
        ),
        in_specs=specs(7),
        out_specs=specs(2),
        scratch_shapes=[
            pltpu.VMEM((n, KV_ROWS, T), BF),
            pltpu.VMEM((2, CHUNKS, N, CW), F32),
            pltpu.VMEM((2, 1, HALF), F32),
            pltpu.VMEM((T, width), F32),
            pltpu.VMEM((T, T), F32),
            chunked, chunked, pltpu.VMEM((1, HALF), F32), chunked, chunked, chunked,
            pltpu.VMEM((2, CHUNKS, N, CW), BF),
            pltpu.VMEM((KVH, big, DH), BF),
            pltpu.VMEM((KVH, big, T), F32),
            pltpu.VMEM((KVH, big, WITH_SUM), F32),
            sem((CHUNKS,)), sem((CHUNKS,)), sem((2,)), sem((CHUNKS,)), sem((CHUNKS,)),
            sem((CHUNKS,)), sem((CHUNKS,)), sem((rows,)), sem((n,)), sem((rows,)),
        ],
        compiler_params=pltpu.CompilerParams(
            collective_id=0, has_side_effects=True, vmem_limit_bytes=VMEM_LIMIT
        ),
        name="mix_and_attend",
    )(mixer_input, input_map, output_map, log_decay.T, query_rows, key_rows.T, value_rows.T)
    return pl.pallas_call(
        deliver_kernel,
        out_shape=(
            jax.ShapeDtypeStruct((T, width), BF),
            jax.ShapeDtypeStruct((T, QH * DH), BF),
        ),
        in_specs=specs(2),
        out_specs=specs(2),
        name="deliver",
    )(mixed, attended)


def solution(mesh):
    rows = P(("dp", "ctx"), None)
    return jax.shard_map(
        functools.partial(per_device, mesh.shape["ctx"]),
        mesh=mesh,
        in_specs=(rows,) * 7,
        out_specs=(rows, rows),
        check_vma=False,
    )
```
